512 devices in a mesh: src: 16 (over y_hi, x, core), tgt: 32 (over z, y_lo).
Axes of the slice: x: 4, y: 4 (y_hi: 2, y_lo: 2; y = y_hi * 2 + y_lo), z: 16, core: 2. Of those that a mesh axis runs over, the one named last changes fastest.
Arguments:
- source: bfloat16 [16384, 64], P('src'), may hold values from -30 to 30
- target: bfloat16 [131072, 64], P('tgt'), may hold values from -6 to 6
- log_source: float32 [32, 16384], P(None, 'src'), may hold values from -6 to 6
- log_target: float32 [32, 131072], P(None, 'tgt'), may hold values from -6 to 6
Outputs:
- src_potential: float32 [32, 16384], P(None, 'src')
- tgt_potential: float32 [32, 131072], P(None, 'tgt')
The draws below stay inside these ranges and needn't reach their ends.
All inputs are finite; a program needn't handle non-finite values.
Results may differ from the reference program's by a relative error of at most 0.00032.
Values sent between devices are 32-bit elements; how exact they have to be, the bound alone decides.
No kernel may reach another device: no remote copies, remote signals or barrier semaphores. Data moves between devices by JAX's collectives and lax.ppermute only.
A program may use at most 64 MiB of HBM per device.

```python
import jax
import jax.numpy as jnp
from jax import lax

FEAT = 64
PAIRS = 32
ITERS = 2
SRC_DEV = 1024
TGT_DEV = 4096
NS = 16384
NT = 131072


def draw_source(key, part):
    key = jax.random.fold_in(key, 3)
    values = jnp.clip(jax.random.normal(key, (NS, FEAT), jnp.float32), -6.0, 6.0)
    return values.astype(jnp.bfloat16)


def levels(own_key, shape, shards, smallest, top_value):
    def one(dim, parts):
        heights = jax.random.uniform(jax.random.fold_in(jax.random.fold_in(own_key, 6), dim), (parts,), jnp.float32, smallest / len(shards), top_value / len(shards))
        return jnp.repeat(jnp.exp(heights), shape[dim] // parts).reshape((-1,) + (1,) * (len(shape) - dim - 1))

    loudness = one(*shards[0])
    for cut in shards[1:]:
        loudness = loudness * one(*cut)
    return loudness


def noise(rng, dims, deviation, bound, split=(), held_as=jnp.bfloat16):
    gain = levels(rng, dims, split, -0.22, 0.18) if split else 1.0
    array = jax.random.normal(rng, dims, jnp.float32) * deviation * gain
    return jnp.minimum(jnp.maximum(array, -bound), bound).astype(held_as)


def setup_inputs(seed: int = 0) -> dict:
    key_list = jax.random.split(jax.random.key(seed), 5)
    source = draw_source(jax.random.fold_in(key_list[4], 71), 0)
    target = noise(key_list[1], (NT, FEAT), 1.0, 6.0, ((0, 32),))
    log_source = noise(key_list[2], (PAIRS, NS), 1.5, 6.0, ((1, 16),), jnp.float32)
    log_target = noise(key_list[3], (PAIRS, NT), 1.5, 6.0, ((1, 32),), jnp.float32)
    return {"source": source, "target": target, "log_source": log_source, "log_target": log_target}


entropy = 0.1


def cost_block(rows, cols):
    row_sq = jnp.sum(jnp.square(rows.astype(jnp.float32)), axis=1)
    col_sq = jnp.sum(jnp.square(cols.astype(jnp.float32)), axis=1)
    cross = jnp.dot(rows, cols.T, preferred_element_type=jnp.float32)
    return (row_sq[:, None] + col_sq[None, :] - 2.0 * cross) / FEAT


def lse_terms(cost, pot):
    top = jnp.max(pot, axis=0)
    shift = top[None, :] - cost / entropy
    peak = jnp.max(shift, axis=1)
    kernel = jnp.exp(shift - peak[:, None]).astype(jnp.bfloat16)
    weight = jnp.exp(pot - top[None, :]).astype(jnp.bfloat16)
    total = lax.dot_general(weight, kernel, (((1,), (1,)), ((), ())), preferred_element_type=jnp.float32)
    return peak, total


def potential(cells, others, other_pot, block):
    count = others.shape[0] // block

    def one(index):
        start = (index * block).astype(jnp.int32)
        part = lax.dynamic_slice_in_dim(others, start, block, 0)
        pot = lax.dynamic_slice_in_dim(other_pot, start, block, 1)
        return lse_terms(cost_block(cells, part), pot)

    peaks, totals = lax.map(one, jnp.arange(count, dtype=jnp.int32))
    best = jnp.max(peaks, axis=0)
    summed = jnp.sum(totals * jnp.exp(peaks - best[None, :])[:, None, :], axis=0)
    return -entropy * (best[None, :] + jnp.log(summed))


def reference(source, target, log_source, log_target):
    tgt_potential = jnp.zeros((PAIRS, NT), jnp.float32)
    src_potential = jnp.zeros((PAIRS, NS), jnp.float32)
    for step in range(ITERS):
        src_potential = potential(source, target, tgt_potential / entropy + log_target, TGT_DEV)
        tgt_potential = potential(target, source, src_potential / entropy + log_source, SRC_DEV)
    return src_potential, tgt_potential
```

```python
import functools
import math

import jax
import jax.numpy as jnp
from jax import lax
from jax.experimental import pallas as pl
from jax.experimental.pallas import tpu as pltpu
from jax.sharding import Mesh
from jax.sharding import PartitionSpec as P

FEAT = 64
ITERS = 2
PAIRS = 32
LANES = 128

entropy = 0.1

LOG2E = math.log2(math.e)
HALF = LOG2E / (FEAT * entropy)
SCALE = 2.0 * HALF
BACK = -entropy / LOG2E

NEAR = ("zl", "yl")
FAR = ("zh",)
SRC = ("yh", "x", "core")

COLS = 256
CHUNK = 512


def pieces(value):
    high = value.astype(jnp.bfloat16)
    rest = value - high.astype(jnp.float32)
    middle = rest.astype(jnp.bfloat16)
    low = (rest - middle.astype(jnp.float32)).astype(jnp.bfloat16)
    return (high, middle, low)


def square_norms(cells):
    square = jnp.square(cells.astype(jnp.float32))
    high = square.astype(jnp.bfloat16)
    low = (square - high.astype(jnp.float32)).astype(jnp.bfloat16)
    both = jnp.concatenate([high, low], axis=1)
    ones = jnp.ones((8, both.shape[1]), jnp.bfloat16)
    sums = lax.dot_general(ones, both, (((1,), (1,)), ((), ())), preferred_element_type=jnp.float32)
    return sums[:1]


def update_kernel(first, emit, *refs):
    refs = list(refs)
    others_ref, cells_ref, log_ref = refs[:3]
    refs = refs[3:]
    known_ref = None if first else refs.pop(0)
    out_ref = refs.pop(0)
    pot_ref = refs.pop(0) if emit else None
    norm_ref = refs.pop(0) if first else None
    left_ref, right_ref, weight_ref = refs

    others = others_ref.shape[0]
    cells = cells_ref.shape[0]
    rows = others // LANES

    scaled = cells_ref[...].astype(jnp.float32) * SCALE
    high, middle, low = pieces(scaled)
    lane = lax.broadcasted_iota(jnp.int32, (cells, FEAT), 1)
    ones = jnp.where(lane < 3, 1.0, 0.0).astype(jnp.bfloat16)
    right_ref[:, :LANES] = jnp.concatenate([high, middle], axis=1)
    right_ref[:, LANES:] = jnp.concatenate([ones, low], axis=1)

    if first or emit:
        norms = square_norms(others_ref[...]) * HALF
    if first:
        norm_ref[...] = jnp.broadcast_to(norms, norm_ref.shape)

    for row in range(rows):
        part = slice(row * LANES, (row + 1) * LANES)
        pot = log_ref[:, part] * LOG2E
        if not first:
            known = known_ref[pl.ds(row, PAIRS, stride=rows), :]
            pot = pot - known
        if emit:
            pot_ref[:, part] = (known - norms[:, part]) * BACK
        top = jnp.max(pot, axis=0, keepdims=True)
        weight_ref[:, part] = jnp.exp2(pot - top).astype(jnp.bfloat16)
        bias = top - norms[:, part] if first else top
        high, middle, low = pieces(bias)
        at = lax.broadcasted_iota(jnp.int32, (8, LANES), 0)
        high, middle, low = (jnp.broadcast_to(x.astype(jnp.float32), (8, LANES)) for x in (high, middle, low))
        block = jnp.where(at == 0, high, jnp.where(at == 1, middle, jnp.where(at == 2, low, 0.0)))
        block = jnp.concatenate([block, jnp.zeros((LANES - 8, LANES), jnp.float32)], axis=0)
        turned = block.T.astype(jnp.bfloat16)
        feats = others_ref[part, :]
        left_ref[part, :LANES] = jnp.concatenate([feats, feats], axis=1)
        left_ref[part, LANES:] = jnp.concatenate([turned[:, :FEAT], feats], axis=1)

    def tile(index, carry):
        start = pl.multiple_of(index * COLS, COLS)
        right = right_ref[pl.ds(start, COLS), :]
        peak = total = None
        for at in range(0, others, CHUNK):
            part = slice(at, at + CHUNK)
            shift = lax.dot_general(
                left_ref[part, :], right, (((1,), (1,)), ((), ())), preferred_element_type=jnp.float32
            )
            best = jnp.max(shift, axis=0, keepdims=True)
            if peak is not None:
                best = jnp.maximum(best, peak)
            kernel = jnp.exp2(shift - best).astype(jnp.bfloat16)
            sums = jnp.dot(weight_ref[:, part], kernel, preferred_element_type=jnp.float32)
            total = sums if peak is None else total * jnp.exp2(peak - best) + sums
            peak = best
        result = peak + jnp.log2(total)
        stride = cells // LANES
        for k in range(COLS // LANES):
            out_ref[pl.ds(index * (COLS // LANES) + k, PAIRS, stride=stride), :] = result[:, k * LANES : (k + 1) * LANES]
        return carry

    lax.fori_loop(0, cells // COLS, tile, 0)


def update(others, cells, log, known=None, emit=False):
    first = known is None
    count, own = others.shape[0], cells.shape[0]
    out = [jax.ShapeDtypeStruct((PAIRS * own // LANES, LANES), jnp.float32)]
    if emit:
        out.append(jax.ShapeDtypeStruct((PAIRS, count), jnp.float32))
    if first:
        out.append(jax.ShapeDtypeStruct((8, count), jnp.float32))
    args = [others, cells, log] + ([] if first else [known])
    return pl.pallas_call(
        functools.partial(update_kernel, first, emit),
        out_shape=out,
        scratch_shapes=[
            pltpu.VMEM((count, 2 * LANES), jnp.bfloat16),
            pltpu.VMEM((own, 2 * LANES), jnp.bfloat16),
            pltpu.VMEM((PAIRS, count), jnp.bfloat16),
        ],
        compiler_params=pltpu.CompilerParams(vmem_limit_bytes=40 * 1024 * 1024),
    )(*args)


def log_sum(parts):
    best = jnp.max(parts, axis=0)
    return best + jnp.log2(jnp.sum(jnp.exp2(parts - best[None]), axis=0))


def exchange(value, axes):
    return lax.all_to_all(value, axes, 0, 0)


def spread(value, axes, count):
    return exchange(jnp.broadcast_to(value[None], (count,) + value.shape), axes)


def over_targets(parts, sizes):
    near = sizes["zl"] * sizes["yl"]
    rows = parts.shape[0]
    mine = log_sum(exchange(parts.reshape(near, rows // near, LANES), NEAR))
    mine = log_sum(spread(mine, FAR, sizes["zh"]))
    return spread(mine, NEAR, near).reshape(rows, LANES)


def over_sources(parts, sizes):
    group = sizes["yh"] * sizes["x"] * sizes["core"]
    rows = parts.shape[0]
    mine = log_sum(exchange(parts.reshape(group, rows // group, LANES), SRC))
    return spread(mine, SRC, group).reshape(rows, LANES)


def body(sizes, source, target, log_source, log_target):
    parts, norms = update(target, source, log_target)
    for step in range(ITERS):
        if step:
            (parts,) = update(target, source, log_target, known)
        known = over_targets(parts, sizes)
        if step < ITERS - 1:
            (parts,) = update(source, target, log_source, known)
        else:
            parts, src_potential = update(source, target, log_source, known, emit=True)
        known = over_sources(parts, sizes)
    tgt_potential = (known.reshape(PAIRS, -1) - norms[:1]) * BACK
    return (src_potential, tgt_potential)


def solution(mesh):
    sizes = {"yh": 2, "x": 4, "core": 2, "zh": 4, "zl": 4, "yl": 2}
    fine = Mesh(mesh.devices.reshape(tuple(sizes.values())), tuple(sizes))
    src, tgt = SRC, FAR + NEAR
    in_specs = (P(src, None), P(tgt, None), P(None, src), P(None, tgt))
    out_specs = (P(None, src), P(None, tgt))
    return jax.shard_map(
        functools.partial(body, sizes), mesh=fine, in_specs=in_specs, out_specs=out_specs, check_vma=False
    )
```

```python
import functools
import math

import jax
import jax.numpy as jnp
from jax import lax
from jax.experimental import pallas as pl
from jax.experimental.pallas import tpu as pltpu
from jax.sharding import Mesh
from jax.sharding import PartitionSpec as P

FEAT = 64
ITERS = 2
PAIRS = 32
LANES = 128
DEPTH = 256

entropy = 0.1

LOG2E = math.log2(math.e)
HALF = LOG2E / (FEAT * entropy)
SCALE = 2.0 * HALF
BACK = -entropy / LOG2E
SMALL = 2.0**-90

NEAR = ("zl", "yl")
FAR = ("zh",)
SRC = ("yh", "x", "core")

TILE = 256
CHUNK = 512


def pieces(value):
    high = value.astype(jnp.bfloat16)
    rest = value - high.astype(jnp.float32)
    middle = rest.astype(jnp.bfloat16)
    low = (rest - middle.astype(jnp.float32)).astype(jnp.bfloat16)
    return (high, middle, low)


def half_norms(feats):
    return jnp.sum(jnp.square(feats.astype(jnp.float32)), axis=0, keepdims=True) * HALF


def fill_left(left_ref, cells_ref):
    for at in range(0, left_ref.shape[0], LANES):
        part = slice(at, at + LANES)
        scaled = cells_ref[:, part].astype(jnp.float32) * SCALE
        row = lax.broadcasted_iota(jnp.int32, (LANES - FEAT, LANES), 0)
        ones = jnp.where(row < 3, 1.0, 0.0)
        high, middle, low = (x.astype(jnp.float32) for x in pieces(scaled))
        left_ref[part, :LANES] = jnp.concatenate([high, middle], axis=0).T.astype(jnp.bfloat16)
        left_ref[part, LANES:] = jnp.concatenate([low, ones], axis=0).T.astype(jnp.bfloat16)


def fill_right(right_ref, others_ref, bias):
    count = others_ref.shape[1]
    feats = others_ref[...]
    for k in range(3):
        right_ref[k * FEAT : (k + 1) * FEAT, :] = feats
    row = lax.broadcasted_iota(jnp.int32, (16, count), 0)
    high, middle, low = (jnp.broadcast_to(x.astype(jnp.float32), (16, count)) for x in pieces(bias))
    block = jnp.where(row == 0, high, jnp.where(row == 1, middle, jnp.where(row == 2, low, 0.0)))
    right_ref[3 * FEAT : 3 * FEAT + 16, :] = block.astype(jnp.bfloat16)
    right_ref[3 * FEAT + 16 :, :] = jnp.zeros((DEPTH - 3 * FEAT - 16, count), jnp.bfloat16)


def as_row(column):
    rows = column.shape[0]
    return jnp.broadcast_to(column, (rows, LANES)).T[:1]


def first_kernel(target_ref, source_ref, log_ref, out_ref, kept_ref, peak_ref, bias_ref, norm_ref,
                 left_ref, right_ref, weight_ref, shift_ref):
    cells, others = kept_ref.shape
    fill_left(left_ref, source_ref)
    norms = half_norms(target_ref[...])
    norm_ref[...] = jnp.broadcast_to(norms, norm_ref.shape)
    pot = log_ref[...] * LOG2E
    top = jnp.max(pot, axis=0, keepdims=True)
    weight_ref[...] = jnp.exp2(pot - top).astype(jnp.bfloat16)
    bias = top - norms
    bias_ref[...] = jnp.broadcast_to(bias, bias_ref.shape)
    fill_right(right_ref, target_ref, bias)

    def scores(tile):
        best = None
        for at in range(0, others, CHUNK):
            part = slice(at, at + CHUNK)
            shift = jnp.dot(left_ref[tile * TILE : (tile + 1) * TILE, :], right_ref[:, part],
                            preferred_element_type=jnp.float32)
            shift_ref[tile % 2, :, part] = shift
            for k in range(0, CHUNK, LANES):
                best = shift[:, k : k + LANES] if best is None else jnp.maximum(best, shift[:, k : k + LANES])
        return jnp.max(best, axis=1, keepdims=True)

    tiles = cells // TILE
    peak = scores(0)
    for tile in range(tiles):
        rows = slice(tile * TILE, (tile + 1) * TILE)
        after = scores(tile + 1) if tile + 1 < tiles else None
        total = None
        for at in range(0, others, CHUNK):
            part = slice(at, at + CHUNK)
            kernel = jnp.exp2(shift_ref[tile % 2, :, part] - peak).astype(jnp.bfloat16)
            kept_ref[rows, part] = kernel
            sums = lax.dot_general(weight_ref[:, part], kernel, (((1,), (1,)), ((), ())),
                                   preferred_element_type=jnp.float32)
            total = sums if total is None else total + sums
        for k in range(TILE // LANES):
            part = slice(tile * TILE + k * LANES, tile * TILE + (k + 1) * LANES)
            row = as_row(peak[k * LANES : (k + 1) * LANES])
            peak_ref[:, part] = jnp.broadcast_to(row, (8, LANES))
            result = row + jnp.log2(total[:, k * LANES : (k + 1) * LANES])
            out_ref[pl.ds(tile * (TILE // LANES) + k, PAIRS, stride=cells // LANES), :] = result
        peak = after


def again(out_ref, cells_ref, others_ref, pot_ref, left_ref, right_ref, weight_ref):
    cells, others = left_ref.shape[0], right_ref.shape[1]
    fill_left(left_ref, cells_ref)
    pot = pot_ref[...]
    top = jnp.max(pot, axis=0, keepdims=True)
    weight_ref[...] = jnp.exp2(pot - top).astype(jnp.bfloat16)
    fill_right(right_ref, others_ref, top)

    def tile(index, carry):
        rows = left_ref[pl.ds(pl.multiple_of(index * LANES, LANES), LANES), :]

        def chunk(step, carry):
            peak, total = carry
            part = pl.ds(pl.multiple_of(step * CHUNK, CHUNK), CHUNK)
            shift = jnp.dot(rows, right_ref[:, part], preferred_element_type=jnp.float32)
            best = jnp.maximum(peak, jnp.broadcast_to(jnp.max(shift, axis=1, keepdims=True), peak.shape))
            kernel = jnp.exp2(shift - best[:, :1]).astype(jnp.bfloat16)
            sums = lax.dot_general(weight_ref[:, part], kernel, (((1,), (1,)), ((), ())),
                                   preferred_element_type=jnp.float32)
            return best, total * jnp.exp2(peak - best).T[:1] + sums

        start = (jnp.full((LANES, LANES), -jnp.inf, jnp.float32), jnp.zeros((PAIRS, LANES), jnp.float32))
        peak, total = lax.fori_loop(0, others // CHUNK, chunk, start)
        out_ref[pl.ds(index, PAIRS, stride=cells // LANES), :] = peak.T[:1] + jnp.log2(total)
        return carry

    lax.fori_loop(0, cells // LANES, tile, 0)


def log_sums_of(known_ref, log_ref, pot_ref):
    rows = log_ref.shape[1] // LANES
    for row in range(rows):
        part = slice(row * LANES, (row + 1) * LANES)
        pot_ref[:, part] = log_ref[:, part] * LOG2E - known_ref[pl.ds(row, PAIRS, stride=rows), :]


def next_kernel(to_source, emit, *refs):
    refs = list(refs)
    cells_ref, others_ref, log_ref, known_ref, kept_ref, peak_ref, bias_ref, out_ref = refs[:8]
    refs = refs[8:]
    pot_out = refs.pop(0) if emit else None
    pot_ref, left_ref, right_ref, weight_ref = refs
    cells, others = left_ref.shape[0], right_ref.shape[1]

    log_sums_of(known_ref, log_ref, pot_ref)
    if emit:
        norms = half_norms(others_ref[...])
        rows = others // LANES
        for row in range(rows):
            part = slice(row * LANES, (row + 1) * LANES)
            pot_out[:, part] = (known_ref[pl.ds(row, PAIRS, stride=rows), :] - norms[:, part]) * BACK
    pot = pot_ref[...]
    scaled = pot - bias_ref[:1] if to_source else pot + peak_ref[:1]
    most = jnp.max(jnp.max(scaled, axis=0, keepdims=True), axis=1, keepdims=True)
    weight_ref[...] = jnp.exp2(scaled - most).astype(jnp.bfloat16)
    least = None
    for at in range(0, cells, TILE):
        if to_source:
            total = lax.dot_general(weight_ref[...], kept_ref[at : at + TILE, :], (((1,), (1,)), ((), ())),
                                    preferred_element_type=jnp.float32)
        else:
            total = jnp.dot(weight_ref[...], kept_ref[:, at : at + TILE], preferred_element_type=jnp.float32)
        least = total if least is None else jnp.minimum(least, total)
        for k in range(TILE // LANES):
            part = slice(at + k * LANES, at + (k + 1) * LANES)
            back = peak_ref[:1, part] if to_source else -bias_ref[:1, part]
            result = (back + most) + jnp.log2(total[:, k * LANES : (k + 1) * LANES])
            out_ref[pl.ds(part.start // LANES, PAIRS, stride=cells // LANES), :] = result
    least = jnp.min(least)

    @pl.when(jnp.logical_not(least >= SMALL))
    def _():
        again(out_ref, cells_ref, others_ref, pot_ref, left_ref, right_ref, weight_ref)


LIMIT = pltpu.CompilerParams(vmem_limit_bytes=28 * 1024 * 1024)


def first_update(target, source, log):
    others, cells = target.shape[1], source.shape[1]
    return pl.pallas_call(
        first_kernel,
        out_shape=[
            jax.ShapeDtypeStruct((PAIRS * cells // LANES, LANES), jnp.float32),
            jax.ShapeDtypeStruct((cells, others), jnp.bfloat16),
            jax.ShapeDtypeStruct((8, cells), jnp.float32),
            jax.ShapeDtypeStruct((8, others), jnp.float32),
            jax.ShapeDtypeStruct((8, others), jnp.float32),
        ],
        scratch_shapes=[
            pltpu.VMEM((cells, DEPTH), jnp.bfloat16),
            pltpu.VMEM((DEPTH, others), jnp.bfloat16),
            pltpu.VMEM((PAIRS, others), jnp.bfloat16),
            pltpu.VMEM((2, TILE, others), jnp.float32),
        ],
        compiler_params=LIMIT,
    )(target, source, log)


def next_update(cells, others, log, known, kept, to_source, emit=False):
    own, count = cells.shape[1], others.shape[1]
    out = [jax.ShapeDtypeStruct((PAIRS * own // LANES, LANES), jnp.float32)]
    if emit:
        out.append(jax.ShapeDtypeStruct((PAIRS, count), jnp.float32))
    return pl.pallas_call(
        functools.partial(next_kernel, to_source, emit),
        out_shape=out,
        scratch_shapes=[
            pltpu.VMEM((PAIRS, count), jnp.float32),
            pltpu.VMEM((own, DEPTH), jnp.bfloat16),
            pltpu.VMEM((DEPTH, count), jnp.bfloat16),
            pltpu.VMEM((PAIRS, count), jnp.bfloat16),
        ],
        compiler_params=LIMIT,
    )(cells, others, log, known, *kept)


def log_sum(parts):
    best = jnp.max(parts, axis=0)
    return best + jnp.log2(jnp.sum(jnp.exp2(parts - best[None]), axis=0))


def exchange(value, axes):
    return lax.all_to_all(value, axes, 0, 0)


def spread(value, axes, count):
    return exchange(jnp.broadcast_to(value[None], (count,) + value.shape), axes)


def over_targets(parts, sizes):
    near = sizes["zl"] * sizes["yl"]
    rows = parts.shape[0]
    mine = log_sum(exchange(parts.reshape(near, rows // near, LANES), NEAR))
    mine = log_sum(spread(mine, FAR, sizes["zh"]))
    return spread(mine, NEAR, near).reshape(rows, LANES)


def over_sources(parts, sizes):
    group = sizes["yh"] * sizes["x"] * sizes["core"]
    rows = parts.shape[0]
    mine = log_sum(exchange(parts.reshape(group, rows // group, LANES), SRC))
    return spread(mine, SRC, group).reshape(rows, LANES)


def body(sizes, source, target, log_source, log_target):
    source, target = source.T, target.T
    parts, *kept, norms = first_update(target, source, log_target)
    for step in range(ITERS):
        if step:
            (parts,) = next_update(source, target, log_target, known, kept, True)
        known = over_targets(parts, sizes)
        last = step == ITERS - 1
        parts, *rest = next_update(target, source, log_source, known, kept, False, emit=last)
        known = over_sources(parts, sizes)
    tgt_potential = (known.reshape(PAIRS, -1) - norms[:1]) * BACK
    return (rest[0], tgt_potential)


def solution(mesh):
    sizes = {"yh": 2, "x": 4, "core": 2, "zh": 4, "zl": 4, "yl": 2}
    fine = Mesh(mesh.devices.reshape(tuple(sizes.values())), tuple(sizes))
    src, tgt = SRC, FAR + NEAR
    in_specs = (P(src, None), P(tgt, None), P(None, src), P(None, tgt))
    out_specs = (P(None, src), P(None, tgt))
    return jax.shard_map(
        functools.partial(body, sizes), mesh=fine, in_specs=in_specs, out_specs=out_specs, check_vma=False
    )
```

```python
import functools
import math

import jax
import jax.numpy as jnp
from jax import lax
from jax.experimental import pallas as pl
from jax.experimental.pallas import tpu as pltpu
from jax.sharding import Mesh
from jax.sharding import PartitionSpec as P

FEAT = 64
ITERS = 2
PAIRS = 32
LANES = 128
DEPTH = 256

entropy = 0.1

LOG2E = math.log2(math.e)
HALF = LOG2E / (FEAT * entropy)
SCALE = 2.0 * HALF
BACK = -entropy / LOG2E
SMALL = 2.0**-90

NEAR = ("zl", "yl")
FAR = ("zh",)
SRC = ("yh", "x", "core")

TILE = 256
CHUNK = 512


def pieces(value):
    high = value.astype(jnp.bfloat16)
    rest = value - high.astype(jnp.float32)
    middle = rest.astype(jnp.bfloat16)
    low = (rest - middle.astype(jnp.float32)).astype(jnp.bfloat16)
    return (high, middle, low)


def half_norms(feats):
    return jnp.sum(jnp.square(feats.astype(jnp.float32)), axis=0, keepdims=True) * HALF


def fill_left(left_ref, cells_ref):
    for at in range(0, left_ref.shape[0], LANES):
        part = slice(at, at + LANES)
        scaled = cells_ref[:, part].astype(jnp.float32) * SCALE
        row = lax.broadcasted_iota(jnp.int32, (LANES - FEAT, LANES), 0)
        ones = jnp.where(row < 3, 1.0, 0.0)
        high, middle, low = (x.astype(jnp.float32) for x in pieces(scaled))
        left_ref[part, :LANES] = jnp.concatenate([high, middle], axis=0).T.astype(jnp.bfloat16)
        left_ref[part, LANES:] = jnp.concatenate([low, ones], axis=0).T.astype(jnp.bfloat16)


def fill_right(right_ref, others_ref, bias):
    count = others_ref.shape[1]
    feats = others_ref[...]
    for k in range(3):
        right_ref[k * FEAT : (k + 1) * FEAT, :] = feats
    row = lax.broadcasted_iota(jnp.int32, (16, count), 0)
    high, middle, low = (jnp.broadcast_to(x.astype(jnp.float32), (16, count)) for x in pieces(bias))
    block = jnp.where(row == 0, high, jnp.where(row == 1, middle, jnp.where(row == 2, low, 0.0)))
    right_ref[3 * FEAT : 3 * FEAT + 16, :] = block.astype(jnp.bfloat16)
    right_ref[3 * FEAT + 16 :, :] = jnp.zeros((DEPTH - 3 * FEAT - 16, count), jnp.bfloat16)


def as_row(column):
    rows = column.shape[0]
    return jnp.broadcast_to(column, (rows, LANES)).T[:1]


def arrive(pairs, sems):
    copies = [pltpu.make_async_copy(src, dst, sems.at[k]) for k, (src, dst) in enumerate(pairs)]
    for copy in copies:
        copy.start()
    return copies


def first_kernel(target_hbm, source_hbm, log_target_hbm, log_source_hbm,
                 out_ref, kept_ref, peak_ref, bias_ref, target_norm_ref, source_norm_ref, log_target_ref,
                 log_source_ref, target_ref, source_ref, left_ref, right_ref, weight_ref, shift_ref, sems):
    cells, others = kept_ref.shape
    copies = arrive(
        [(source_hbm, source_ref), (log_target_hbm, log_target_ref), (target_hbm, target_ref),
         (log_source_hbm, log_source_ref)],
        sems,
    )
    copies[0].wait()
    fill_left(left_ref, source_ref)
    source_norm_ref[...] = jnp.broadcast_to(half_norms(source_ref[...]), source_norm_ref.shape)
    copies[1].wait()
    pot = log_target_ref[...] * LOG2E
    top = jnp.max(pot, axis=0, keepdims=True)
    weight_ref[...] = jnp.exp2(pot - top).astype(jnp.bfloat16)
    copies[2].wait()
    norms = half_norms(target_ref[...])
    target_norm_ref[...] = jnp.broadcast_to(norms, target_norm_ref.shape)
    bias = top - norms
    bias_ref[...] = jnp.broadcast_to(bias, bias_ref.shape)
    fill_right(right_ref, target_ref, bias)

    def scores(tile):
        best = None
        for at in range(0, others, CHUNK):
            part = slice(at, at + CHUNK)
            shift = jnp.dot(left_ref[tile * TILE : (tile + 1) * TILE, :], right_ref[:, part],
                            preferred_element_type=jnp.float32)
            shift_ref[tile % 2, :, part] = shift
            for k in range(0, CHUNK, LANES):
                best = shift[:, k : k + LANES] if best is None else jnp.maximum(best, shift[:, k : k + LANES])
        return jnp.max(best, axis=1, keepdims=True)

    tiles = cells // TILE
    peak = scores(0)
    for tile in range(tiles):
        rows = slice(tile * TILE, (tile + 1) * TILE)
        after = scores(tile + 1) if tile + 1 < tiles else None
        total = None
        for at in range(0, others, CHUNK):
            part = slice(at, at + CHUNK)
            kernel = jnp.exp2(shift_ref[tile % 2, :, part] - peak).astype(jnp.bfloat16)
            kept_ref[rows, part] = kernel
            sums = lax.dot_general(weight_ref[:, part], kernel, (((1,), (1,)), ((), ())),
                                   preferred_element_type=jnp.float32)
            total = sums if total is None else total + sums
        for k in range(TILE // LANES):
            part = slice(tile * TILE + k * LANES, tile * TILE + (k + 1) * LANES)
            row = as_row(peak[k * LANES : (k + 1) * LANES])
            peak_ref[:, part] = jnp.broadcast_to(row, (8, LANES))
            result = row + jnp.log2(total[:, k * LANES : (k + 1) * LANES])
            out_ref[pl.ds(tile * (TILE // LANES) + k, PAIRS, stride=cells // LANES), :] = result
        peak = after
    copies[3].wait()


def again(out_ref, cells_ref, others_ref, pot_ref, left_ref, right_ref, weight_ref):
    cells, others = left_ref.shape[0], right_ref.shape[1]
    fill_left(left_ref, cells_ref)
    pot = pot_ref[...]
    top = jnp.max(pot, axis=0, keepdims=True)
    weight_ref[...] = jnp.exp2(pot - top).astype(jnp.bfloat16)
    fill_right(right_ref, others_ref, top)

    def tile(index, carry):
        rows = left_ref[pl.ds(pl.multiple_of(index * LANES, LANES), LANES), :]

        def chunk(step, carry):
            peak, total = carry
            part = pl.ds(pl.multiple_of(step * CHUNK, CHUNK), CHUNK)
            shift = jnp.dot(rows, right_ref[:, part], preferred_element_type=jnp.float32)
            best = jnp.maximum(peak, jnp.broadcast_to(jnp.max(shift, axis=1, keepdims=True), peak.shape))
            kernel = jnp.exp2(shift - best[:, :1]).astype(jnp.bfloat16)
            sums = lax.dot_general(weight_ref[:, part], kernel, (((1,), (1,)), ((), ())),
                                   preferred_element_type=jnp.float32)
            return best, total * jnp.exp2(peak - best).T[:1] + sums

        start = (jnp.full((LANES, LANES), -jnp.inf, jnp.float32), jnp.zeros((PAIRS, LANES), jnp.float32))
        peak, total = lax.fori_loop(0, others // CHUNK, chunk, start)
        out_ref[pl.ds(index, PAIRS, stride=cells // LANES), :] = peak.T[:1] + jnp.log2(total)
        return carry

    lax.fori_loop(0, cells // LANES, tile, 0)


def log_sums_of(known_ref, log_ref, pot_ref):
    rows = log_ref.shape[1] // LANES
    for row in range(rows):
        part = slice(row * LANES, (row + 1) * LANES)
        pot_ref[:, part] = log_ref[:, part] * LOG2E - known_ref[pl.ds(row, PAIRS, stride=rows), :]


def next_kernel(to_source, emit, *refs):
    refs = list(refs)
    cells_hbm, others_hbm, log_ref, known_ref, kept_ref, peak_ref, bias_ref = refs[:7]
    refs = refs[7:]
    norm_ref = refs.pop(0) if emit else None
    out_ref = refs.pop(0)
    pot_out = refs.pop(0) if emit else None
    cells_ref, others_ref, pot_ref, left_ref, right_ref, weight_ref, sems = refs
    cells, others = left_ref.shape[0], right_ref.shape[1]

    log_sums_of(known_ref, log_ref, pot_ref)
    if emit:
        rows = others // LANES
        for row in range(rows):
            part = slice(row * LANES, (row + 1) * LANES)
            pot_out[:, part] = (known_ref[pl.ds(row, PAIRS, stride=rows), :] - norm_ref[:1, part]) * BACK
    pot = pot_ref[...]
    scaled = pot - bias_ref[:1] if to_source else pot + peak_ref[:1]
    most = jnp.max(jnp.max(scaled, axis=0, keepdims=True), axis=1, keepdims=True)
    weight_ref[...] = jnp.exp2(scaled - most).astype(jnp.bfloat16)
    least = None
    for at in range(0, cells, TILE):
        if to_source:
            total = lax.dot_general(weight_ref[...], kept_ref[at : at + TILE, :], (((1,), (1,)), ((), ())),
                                    preferred_element_type=jnp.float32)
        else:
            total = jnp.dot(weight_ref[...], kept_ref[:, at : at + TILE], preferred_element_type=jnp.float32)
        least = total if least is None else jnp.minimum(least, total)
        for k in range(TILE // LANES):
            part = slice(at + k * LANES, at + (k + 1) * LANES)
            back = peak_ref[:1, part] if to_source else -bias_ref[:1, part]
            result = (back + most) + jnp.log2(total[:, k * LANES : (k + 1) * LANES])
            out_ref[pl.ds(part.start // LANES, PAIRS, stride=cells // LANES), :] = result
    least = jnp.min(least)

    @pl.when(jnp.logical_not(least >= SMALL))
    def _():
        for copy in arrive([(cells_hbm, cells_ref), (others_hbm, others_ref)], sems):
            copy.wait()
        again(out_ref, cells_ref, others_ref, pot_ref, left_ref, right_ref, weight_ref)


LIMIT = pltpu.CompilerParams(vmem_limit_bytes=24 * 1024 * 1024)
HBM = pl.BlockSpec(memory_space=pltpu.HBM)
VMEM = pl.BlockSpec(memory_space=pltpu.VMEM)


def in_hbm(*arrays):
    return [pltpu.with_memory_space_constraint(array, pltpu.HBM) for array in arrays]


def first_update(target, source, log_target, log_source):
    others, cells = target.shape[1], source.shape[1]
    return pl.pallas_call(
        first_kernel,
        out_shape=[
            jax.ShapeDtypeStruct((PAIRS * cells // LANES, LANES), jnp.float32),
            jax.ShapeDtypeStruct((cells, others), jnp.bfloat16),
            jax.ShapeDtypeStruct((8, cells), jnp.float32),
            jax.ShapeDtypeStruct((8, others), jnp.float32),
            jax.ShapeDtypeStruct((8, others), jnp.float32),
            jax.ShapeDtypeStruct((8, cells), jnp.float32),
            jax.ShapeDtypeStruct(log_target.shape, log_target.dtype),
            jax.ShapeDtypeStruct(log_source.shape, log_source.dtype),
        ],
        in_specs=[HBM] * 4,
        out_specs=[VMEM] * 8,
        scratch_shapes=[
            pltpu.VMEM(target.shape, target.dtype),
            pltpu.VMEM(source.shape, source.dtype),
            pltpu.VMEM((cells, DEPTH), jnp.bfloat16),
            pltpu.VMEM((DEPTH, others), jnp.bfloat16),
            pltpu.VMEM((PAIRS, others), jnp.bfloat16),
            pltpu.VMEM((2, TILE, others), jnp.float32),
            pltpu.SemaphoreType.DMA((4,)),
        ],
        compiler_params=LIMIT,
    )(*in_hbm(target, source, log_target, log_source))


def next_update(cells, others, log, known, kept, to_source, norms=None):
    own, count = cells.shape[1], others.shape[1]
    emit = norms is not None
    out = [jax.ShapeDtypeStruct((PAIRS * own // LANES, LANES), jnp.float32)]
    args = [*in_hbm(cells, others), log, known, *kept]
    if emit:
        out.append(jax.ShapeDtypeStruct((PAIRS, count), jnp.float32))
        args.append(norms)
    return pl.pallas_call(
        functools.partial(next_kernel, to_source, emit),
        out_shape=out,
        in_specs=[HBM] * 2 + [VMEM] * (len(args) - 2),
        out_specs=[VMEM] * len(out),
        scratch_shapes=[
            pltpu.VMEM(cells.shape, cells.dtype),
            pltpu.VMEM(others.shape, others.dtype),
            pltpu.VMEM((PAIRS, count), jnp.float32),
            pltpu.VMEM((own, DEPTH), jnp.bfloat16),
            pltpu.VMEM((DEPTH, count), jnp.bfloat16),
            pltpu.VMEM((PAIRS, count), jnp.bfloat16),
            pltpu.SemaphoreType.DMA((2,)),
        ],
        compiler_params=LIMIT,
    )(*args)


def log_sum(parts):
    best = jnp.max(parts, axis=0)
    return best + jnp.log2(jnp.sum(jnp.exp2(parts - best[None]), axis=0))


def combine_kernel(parts_ref, out_ref):
    out_ref[...] = jnp.broadcast_to(log_sum(parts_ref[...])[None], out_ref.shape)


def combine(parts, copies):
    return pl.pallas_call(
        combine_kernel,
        out_shape=jax.ShapeDtypeStruct((copies,) + parts.shape[1:], jnp.float32),
        compiler_params=pltpu.CompilerParams(vmem_limit_bytes=4 * 1024 * 1024),
    )(parts)


def finish_kernel(known_ref, norm_ref, out_ref):
    rows = out_ref.shape[1] // LANES
    for row in range(rows):
        part = slice(row * LANES, (row + 1) * LANES)
        out_ref[:, part] = (known_ref[pl.ds(row, PAIRS, stride=rows), :] - norm_ref[:1, part]) * BACK


def finish(known, norms):
    return pl.pallas_call(
        finish_kernel,
        out_shape=jax.ShapeDtypeStruct((PAIRS, norms.shape[1]), jnp.float32),
        compiler_params=pltpu.CompilerParams(vmem_limit_bytes=4 * 1024 * 1024),
    )(known, norms)


def exchange(value, axes):
    return lax.all_to_all(value, axes, 0, 0)


def over_targets(parts, sizes):
    near = sizes["zl"] * sizes["yl"]
    rows = parts.shape[0]
    mine = exchange(parts.reshape(near, rows // near, LANES), NEAR)
    mine = exchange(combine(mine, sizes["zh"]), FAR)
    return exchange(combine(mine, near), NEAR).reshape(rows, LANES)


def over_sources(parts, sizes):
    group = sizes["yh"] * sizes["x"] * sizes["core"]
    rows = parts.shape[0]
    mine = exchange(parts.reshape(group, rows // group, LANES), SRC)
    return exchange(combine(mine, group), SRC).reshape(rows, LANES)


def body(sizes, source, target, log_source, log_target):
    source, target = source.T, target.T
    parts, *kept, target_norms, source_norms, log_target, log_source = first_update(
        target, source, log_target, log_source
    )
    for step in range(ITERS):
        if step:
            (parts,) = next_update(source, target, log_target, known, kept, True)
        known = over_targets(parts, sizes)
        norms = source_norms if step == ITERS - 1 else None
        parts, *rest = next_update(target, source, log_source, known, kept, False, norms)
        known = over_sources(parts, sizes)
    return (rest[0], finish(known, target_norms))


def solution(mesh):
    sizes = {"yh": 2, "x": 4, "core": 2, "zh": 4, "zl": 4, "yl": 2}
    fine = Mesh(mesh.devices.reshape(tuple(sizes.values())), tuple(sizes))
    src, tgt = SRC, FAR + NEAR
    in_specs = (P(src, None), P(tgt, None), P(None, src), P(None, tgt))
    out_specs = (P(None, src), P(None, tgt))
    return jax.shard_map(
        functools.partial(body, sizes), mesh=fine, in_specs=in_specs, out_specs=out_specs, check_vma=False
    )
```

```python
import functools
import math

import jax
import jax.numpy as jnp
from jax import lax
from jax.experimental import pallas as pl
from jax.experimental.pallas import tpu as pltpu
from jax.sharding import Mesh
from jax.sharding import PartitionSpec as P

FEAT = 64
ITERS = 2
PAIRS = 32
LANES = 128
GROUP = 8
DEPTH = 256

entropy = 0.1

LOG2E = math.log2(math.e)
HALF = LOG2E / (FEAT * entropy)
SCALE = 2.0 * HALF
BACK = -entropy / LOG2E
SMALL = 2.0**-90

NEAR = ("zl", "yl")
FAR = ("zh",)
CHIPS = ("yh", "x")
SRC = CHIPS + ("core",)

TILE = 256
CHUNK = 512


def pieces(value):
    high = value.astype(jnp.bfloat16)
    rest = value - high.astype(jnp.float32)
    middle = rest.astype(jnp.bfloat16)
    low = (rest - middle.astype(jnp.float32)).astype(jnp.bfloat16)
    return (high, middle, low)


def half_norms(feats):
    return jnp.sum(jnp.square(feats.astype(jnp.float32)), axis=0, keepdims=True) * HALF


def fill_left(left_ref, cells_ref):
    for at in range(0, left_ref.shape[0], LANES):
        part = slice(at, at + LANES)
        scaled = cells_ref[:, part].astype(jnp.float32) * SCALE
        row = lax.broadcasted_iota(jnp.int32, (LANES - FEAT, LANES), 0)
        ones = jnp.where(row < 3, 1.0, 0.0)
        high, middle, low = (x.astype(jnp.float32) for x in pieces(scaled))
        left_ref[part, :LANES] = jnp.concatenate([high, middle], axis=0).T.astype(jnp.bfloat16)
        left_ref[part, LANES:] = jnp.concatenate([low, ones], axis=0).T.astype(jnp.bfloat16)


def fill_right(right_ref, others_ref, bias):
    count = others_ref.shape[1]
    feats = others_ref[...]
    for k in range(3):
        right_ref[k * FEAT : (k + 1) * FEAT, :] = feats
    row = lax.broadcasted_iota(jnp.int32, (16, count), 0)
    high, middle, low = (jnp.broadcast_to(x.astype(jnp.float32), (16, count)) for x in pieces(bias))
    block = jnp.where(row == 0, high, jnp.where(row == 1, middle, jnp.where(row == 2, low, 0.0)))
    right_ref[3 * FEAT : 3 * FEAT + 16, :] = block.astype(jnp.bfloat16)
    right_ref[3 * FEAT + 16 :, :] = jnp.zeros((DEPTH - 3 * FEAT - 16, count), jnp.bfloat16)


def tile_rows(group, column, count):
    return slice((group * (count // LANES) + column) * GROUP, (group * (count // LANES) + column + 1) * GROUP)


def as_row(column):
    rows = column.shape[0]
    return jnp.broadcast_to(column, (rows, LANES)).T[:1]


def arrive(pairs, sems):
    copies = [pltpu.make_async_copy(src, dst, sems.at[k]) for k, (src, dst) in enumerate(pairs)]
    for copy in copies:
        copy.start()
    return copies


def first_kernel(target_hbm, source_hbm, log_target_hbm, log_source_hbm,
                 out_ref, kept_ref, peak_ref, bias_ref, target_norm_ref, source_norm_ref, log_target_ref,
                 log_source_ref, target_ref, source_ref, left_ref, right_ref, weight_ref, shift_ref, sems):
    cells, others = kept_ref.shape
    copies = arrive(
        [(source_hbm, source_ref), (log_target_hbm, log_target_ref), (target_hbm, target_ref),
         (log_source_hbm, log_source_ref)],
        sems,
    )
    copies[0].wait()
    fill_left(left_ref, source_ref)
    source_norm_ref[...] = jnp.broadcast_to(half_norms(source_ref[...]), source_norm_ref.shape)
    copies[1].wait()
    pot = log_target_ref[...] * LOG2E
    top = jnp.max(pot, axis=0, keepdims=True)
    weight_ref[...] = jnp.exp2(pot - top).astype(jnp.bfloat16)
    copies[2].wait()
    norms = half_norms(target_ref[...])
    target_norm_ref[...] = jnp.broadcast_to(norms, target_norm_ref.shape)
    bias = top - norms
    bias_ref[...] = jnp.broadcast_to(bias, bias_ref.shape)
    fill_right(right_ref, target_ref, bias)

    def scores(tile):
        best = None
        for at in range(0, others, CHUNK):
            part = slice(at, at + CHUNK)
            shift = jnp.dot(left_ref[tile * TILE : (tile + 1) * TILE, :], right_ref[:, part],
                            preferred_element_type=jnp.float32)
            shift_ref[tile % 2, :, part] = shift
            for k in range(0, CHUNK, LANES):
                best = shift[:, k : k + LANES] if best is None else jnp.maximum(best, shift[:, k : k + LANES])
        return jnp.max(best, axis=1, keepdims=True)

    tiles = cells // TILE
    peak = scores(0)
    for tile in range(tiles):
        rows = slice(tile * TILE, (tile + 1) * TILE)
        after = scores(tile + 1) if tile + 1 < tiles else None
        total = None
        for at in range(0, others, CHUNK):
            part = slice(at, at + CHUNK)
            kernel = jnp.exp2(shift_ref[tile % 2, :, part] - peak).astype(jnp.bfloat16)
            kept_ref[rows, part] = kernel
            sums = lax.dot_general(weight_ref[:, part], kernel, (((1,), (1,)), ((), ())),
                                   preferred_element_type=jnp.float32)
            total = sums if total is None else total + sums
        for k in range(TILE // LANES):
            part = slice(tile * TILE + k * LANES, tile * TILE + (k + 1) * LANES)
            row = jnp.broadcast_to(as_row(peak[k * LANES : (k + 1) * LANES]), (GROUP, LANES))
            peak_ref[:, part] = row
            result = jnp.log2(total[:, k * LANES : (k + 1) * LANES])
            for group in range(PAIRS // GROUP):
                place = tile_rows(group, tile * (TILE // LANES) + k, cells)
                out_ref[place, :] = row + result[group * GROUP : (group + 1) * GROUP]
        peak = after
    copies[3].wait()


def again(put, cells_ref, others_ref, log_ref, known_ref, pot_ref, left_ref, right_ref, weight_ref):
    cells, others = left_ref.shape[0], right_ref.shape[1]
    fill_left(left_ref, cells_ref)
    potentials(log_ref, known_ref, pot_ref)
    pot = pot_ref[...]
    top = jnp.max(pot, axis=0, keepdims=True)
    weight_ref[...] = jnp.exp2(pot - top).astype(jnp.bfloat16)
    fill_right(right_ref, others_ref, top)

    def tile(index, carry):
        rows = left_ref[pl.ds(pl.multiple_of(index * LANES, LANES), LANES), :]

        def chunk(step, carry):
            peak, total = carry
            part = pl.ds(pl.multiple_of(step * CHUNK, CHUNK), CHUNK)
            shift = jnp.dot(rows, right_ref[:, part], preferred_element_type=jnp.float32)
            best = jnp.maximum(peak, jnp.broadcast_to(jnp.max(shift, axis=1, keepdims=True), peak.shape))
            kernel = jnp.exp2(shift - best[:, :1]).astype(jnp.bfloat16)
            sums = lax.dot_general(weight_ref[:, part], kernel, (((1,), (1,)), ((), ())),
                                   preferred_element_type=jnp.float32)
            return best, total * jnp.exp2(peak - best).T[:1] + sums

        start = (jnp.full((LANES, LANES), -jnp.inf, jnp.float32), jnp.zeros((PAIRS, LANES), jnp.float32))
        peak, total = lax.fori_loop(0, others // CHUNK, chunk, start)
        put(index, peak.T[:1] + jnp.log2(total))
        return carry

    lax.fori_loop(0, cells // LANES, tile, 0)


def potentials(log_ref, known_ref, pot_ref, add=None):
    count = log_ref.shape[1]
    most = None
    for column in range(count // LANES):
        part = slice(column * LANES, (column + 1) * LANES)
        row = 0.0 if add is None else add(part)
        for group in range(PAIRS // GROUP):
            pairs = slice(group * GROUP, (group + 1) * GROUP)
            value = log_ref[pairs, part] * LOG2E - known_ref[tile_rows(group, column, count), :] + row
            pot_ref[pairs, part] = value
            most = value if most is None else jnp.maximum(most, value)
    return jnp.max(jnp.max(most, axis=0, keepdims=True), axis=1, keepdims=True)


def next_kernel(to_source, *refs):
    cells_hbm, others_hbm, log_ref, known_ref, kept_ref, peak_ref, bias_ref = refs[:7]
    outs = refs[7:8] if to_source else refs[7:9]
    cells_ref, others_ref, pot_ref, left_ref, right_ref, weight_ref, sems = refs[7 + len(outs) :]
    cells, others = left_ref.shape[0], right_ref.shape[1]
    groups = PAIRS // GROUP

    if to_source:
        most = potentials(log_ref, known_ref, pot_ref, lambda part: -bias_ref[:, part])

        def put(column, result):
            for group in range(groups):
                place = pl.ds((group * (cells // LANES) + column) * GROUP, GROUP)
                outs[0][place, :] = result[group * GROUP : (group + 1) * GROUP]
    else:
        most = potentials(log_ref, known_ref, pot_ref, lambda part: peak_ref[:, part])
        lower = lax.axis_index("core") == 0

        def put(column, result):
            for group in range(groups // 2):
                place = pl.ds((group * (cells // LANES) + column) * GROUP, GROUP)
                low = result[group * GROUP : (group + 1) * GROUP]
                high = result[(group + groups // 2) * GROUP : (group + groups // 2 + 1) * GROUP]
                outs[0][place, :] = jnp.where(lower, low, high)
                outs[1][place, :] = jnp.where(lower, high, low)

    weight_ref[...] = jnp.exp2(pot_ref[...] - most).astype(jnp.bfloat16)
    least = None
    for at in range(0, cells, TILE):
        if to_source:
            total = lax.dot_general(weight_ref[...], kept_ref[at : at + TILE, :], (((1,), (1,)), ((), ())),
                                    preferred_element_type=jnp.float32)
        else:
            total = jnp.dot(weight_ref[...], kept_ref[:, at : at + TILE], preferred_element_type=jnp.float32)
        least = total if least is None else jnp.minimum(least, total)
        for k in range(TILE // LANES):
            part = slice(at + k * LANES, at + (k + 1) * LANES)
            back = peak_ref[:1, part] if to_source else -bias_ref[:1, part]
            put(part.start // LANES, (back + most) + jnp.log2(total[:, k * LANES : (k + 1) * LANES]))
    least = jnp.min(least)

    @pl.when(jnp.logical_not(least >= SMALL))
    def _():
        for copy in arrive([(cells_hbm, cells_ref), (others_hbm, others_ref)], sems):
            copy.wait()
        again(put, cells_ref, others_ref, log_ref, known_ref, pot_ref, left_ref, right_ref, weight_ref)


LIMIT = pltpu.CompilerParams(vmem_limit_bytes=24 * 1024 * 1024)
HBM = pl.BlockSpec(memory_space=pltpu.HBM)
VMEM = pl.BlockSpec(memory_space=pltpu.VMEM)


def in_hbm(*arrays):
    return [pltpu.with_memory_space_constraint(array, pltpu.HBM) for array in arrays]


def first_update(target, source, log_target, log_source):
    others, cells = target.shape[1], source.shape[1]
    return pl.pallas_call(
        first_kernel,
        out_shape=[
            jax.ShapeDtypeStruct((PAIRS * cells // LANES, LANES), jnp.float32),
            jax.ShapeDtypeStruct((cells, others), jnp.bfloat16),
            jax.ShapeDtypeStruct((8, cells), jnp.float32),
            jax.ShapeDtypeStruct((8, others), jnp.float32),
            jax.ShapeDtypeStruct((8, others), jnp.float32),
            jax.ShapeDtypeStruct((8, cells), jnp.float32),
            jax.ShapeDtypeStruct(log_target.shape, log_target.dtype),
            jax.ShapeDtypeStruct(log_source.shape, log_source.dtype),
        ],
        in_specs=[HBM] * 4,
        out_specs=[VMEM] * 8,
        scratch_shapes=[
            pltpu.VMEM(target.shape, target.dtype),
            pltpu.VMEM(source.shape, source.dtype),
            pltpu.VMEM((cells, DEPTH), jnp.bfloat16),
            pltpu.VMEM((DEPTH, others), jnp.bfloat16),
            pltpu.VMEM((PAIRS, others), jnp.bfloat16),
            pltpu.VMEM((2, TILE, others), jnp.float32),
            pltpu.SemaphoreType.DMA((4,)),
        ],
        compiler_params=LIMIT,
    )(*in_hbm(target, source, log_target, log_source))


def next_update(cells, others, log, known, kept, to_source):
    own, count = cells.shape[1], others.shape[1]
    halves = 1 if to_source else 2
    return pl.pallas_call(
        functools.partial(next_kernel, to_source),
        out_shape=[jax.ShapeDtypeStruct((PAIRS * own // LANES // halves, LANES), jnp.float32)] * halves,
        in_specs=[HBM] * 2 + [VMEM] * (2 + len(kept)),
        out_specs=[VMEM] * halves,
        scratch_shapes=[
            pltpu.VMEM(cells.shape, cells.dtype),
            pltpu.VMEM(others.shape, others.dtype),
            pltpu.VMEM((PAIRS, count), jnp.float32),
            pltpu.VMEM((own, DEPTH), jnp.bfloat16),
            pltpu.VMEM((DEPTH, count), jnp.bfloat16),
            pltpu.VMEM((PAIRS, count), jnp.bfloat16),
            pltpu.SemaphoreType.DMA((2,)),
        ],
        compiler_params=LIMIT,
    )(*in_hbm(cells, others), log, known, *kept)


def log_sum(parts):
    best = jnp.max(parts, axis=0)
    return best + jnp.log2(jnp.sum(jnp.exp2(parts - best[None]), axis=0))


def combine_kernel(parts_ref, out_ref):
    out_ref[...] = jnp.broadcast_to(log_sum(parts_ref[...])[None], out_ref.shape)


def combine(parts, copies):
    return pl.pallas_call(
        combine_kernel,
        out_shape=jax.ShapeDtypeStruct((copies,) + parts.shape[1:], jnp.float32),
        compiler_params=pltpu.CompilerParams(vmem_limit_bytes=4 * 1024 * 1024),
    )(parts)


def join_kernel(mine_ref, others_ref, out_ref):
    mine = mine_ref[...]
    other = jnp.where(lax.axis_index("core") == 0, others_ref[1], others_ref[0])
    best = jnp.maximum(mine, other)
    out_ref[...] = best + jnp.log2(jnp.exp2(mine - best) + jnp.exp2(other - best))


def join(mine, others):
    return pl.pallas_call(
        join_kernel,
        out_shape=jax.ShapeDtypeStruct(mine.shape, jnp.float32),
        compiler_params=pltpu.CompilerParams(vmem_limit_bytes=4 * 1024 * 1024),
    )(mine, others)


def finish_kernel(*refs):
    inputs, outs, values, sems = refs[:4], refs[4:6], refs[6:8], refs[8]
    saves = []
    for side in range(2):
        known_ref, norm_ref = inputs[2 * side : 2 * side + 2]
        count = norm_ref.shape[1]
        for group in range(PAIRS // GROUP):
            pairs = slice(group * GROUP, (group + 1) * GROUP)
            for column in range(count // LANES):
                part = slice(column * LANES, (column + 1) * LANES)
                known = known_ref[tile_rows(group, column, count), :]
                values[side][pairs, part] = (known - norm_ref[:, part]) * BACK
            save = pltpu.make_async_copy(values[side].at[pairs], outs[side].at[pairs], sems.at[len(saves)])
            save.start()
            saves.append(save)
    for save in saves:
        save.wait()


def finish(source_known, source_norms, target_known, target_norms):
    shapes = [(PAIRS, norms.shape[1]) for norms in (source_norms, target_norms)]
    return pl.pallas_call(
        finish_kernel,
        out_shape=[jax.ShapeDtypeStruct(shape, jnp.float32) for shape in shapes],
        out_specs=[HBM] * 2,
        scratch_shapes=[pltpu.VMEM(shape, jnp.float32) for shape in shapes]
        + [pltpu.SemaphoreType.DMA((2 * PAIRS // GROUP,))],
        compiler_params=pltpu.CompilerParams(vmem_limit_bytes=4 * 1024 * 1024),
    )(source_known, source_norms, target_known, target_norms)


def exchange(value, axes):
    return lax.all_to_all(value, axes, 0, 0)


def over_targets(parts, sizes):
    near = sizes["zl"] * sizes["yl"]
    rows = parts.shape[0]
    mine = exchange(parts.reshape(near, rows // near, LANES), NEAR)
    mine = exchange(combine(mine, sizes["zh"]), FAR)
    return exchange(combine(mine, near), NEAR).reshape(rows, LANES)


def over_sources(mine, other, sizes):
    group = sizes["yh"] * sizes["x"]
    rows = mine.shape[0]
    mine = join(mine, lax.all_gather(other, "core"))
    mine = exchange(mine.reshape(group, rows // group, LANES), CHIPS)
    half = exchange(combine(mine, group), CHIPS).reshape(rows, LANES)
    return lax.all_gather(half, "core").reshape(2 * rows, LANES)


def body(sizes, source, target, log_source, log_target):
    source, target = source.T, target.T
    parts, *kept, target_norms, source_norms, log_target, log_source = first_update(
        target, source, log_target, log_source
    )
    for step in range(ITERS):
        if step:
            (parts,) = next_update(source, target, log_target, target_known, kept, True)
        source_known = over_targets(parts, sizes)
        target_known = over_sources(*next_update(target, source, log_source, source_known, kept, False), sizes)
    return finish(source_known, source_norms, target_known, target_norms)


def solution(mesh):
    sizes = {"yh": 2, "x": 4, "core": 2, "zh": 4, "zl": 4, "yl": 2}
    fine = Mesh(mesh.devices.reshape(tuple(sizes.values())), tuple(sizes))
    src, tgt = SRC, FAR + NEAR
    in_specs = (P(src, None), P(tgt, None), P(None, src), P(None, tgt))
    out_specs = (P(None, src), P(None, tgt))
    return jax.shard_map(
        functools.partial(body, sizes), mesh=fine, in_specs=in_specs, out_specs=out_specs, check_vma=False
    )
```

```python
import functools
import math

import jax
import jax.numpy as jnp
from jax import lax
from jax.experimental import pallas as pl
from jax.experimental.pallas import tpu as pltpu
from jax.sharding import Mesh
from jax.sharding import PartitionSpec as P

FEAT = 64
ITERS = 2
PAIRS = 32
LANES = 128
GROUP = 8
DEPTH = 256

entropy = 0.1

LOG2E = math.log2(math.e)
HALF = LOG2E / (FEAT * entropy)
SCALE = 2.0 * HALF
BACK = -entropy / LOG2E
SMALL = 2.0**-90

NEAR = ("z0", "yl", "z1")
FAR = ("z2", "z3")
CHIPS = ("x", "yh")

TILE = 256
CHUNK = 512


def pieces(value):
    high = value.astype(jnp.bfloat16)
    rest = value - high.astype(jnp.float32)
    middle = rest.astype(jnp.bfloat16)
    low = (rest - middle.astype(jnp.float32)).astype(jnp.bfloat16)
    return (high, middle, low)


def half_norms(feats):
    return jnp.sum(jnp.square(feats.astype(jnp.float32)), axis=0, keepdims=True) * HALF


def fill_left(left_ref, cells_ref):
    for at in range(0, left_ref.shape[0], LANES):
        part = slice(at, at + LANES)
        scaled = cells_ref[:, part].astype(jnp.float32) * SCALE
        row = lax.broadcasted_iota(jnp.int32, (LANES - FEAT, LANES), 0)
        ones = jnp.where(row < 3, 1.0, 0.0)
        high, middle, low = (x.astype(jnp.float32) for x in pieces(scaled))
        left_ref[part, :LANES] = jnp.concatenate([high, middle], axis=0).T.astype(jnp.bfloat16)
        left_ref[part, LANES:] = jnp.concatenate([low, ones], axis=0).T.astype(jnp.bfloat16)


def fill_right(right_ref, others_ref, bias):
    count = others_ref.shape[1]
    feats = others_ref[...]
    for k in range(3):
        right_ref[k * FEAT : (k + 1) * FEAT, :] = feats
    row = lax.broadcasted_iota(jnp.int32, (16, count), 0)
    high, middle, low = (jnp.broadcast_to(x.astype(jnp.float32), (16, count)) for x in pieces(bias))
    block = jnp.where(row == 0, high, jnp.where(row == 1, middle, jnp.where(row == 2, low, 0.0)))
    right_ref[3 * FEAT : 3 * FEAT + 16, :] = block.astype(jnp.bfloat16)
    right_ref[3 * FEAT + 16 :, :] = jnp.zeros((DEPTH - 3 * FEAT - 16, count), jnp.bfloat16)


def tile_rows(group, column, count):
    return slice((group * (count // LANES) + column) * GROUP, (group * (count // LANES) + column + 1) * GROUP)


def as_row(column):
    rows = column.shape[0]
    return jnp.broadcast_to(column, (rows, LANES)).T[:1]


def arrive(pairs, sems):
    copies = [pltpu.make_async_copy(src, dst, sems.at[k]) for k, (src, dst) in enumerate(pairs)]
    for copy in copies:
        copy.start()
    return copies


def first_kernel(target_hbm, source_hbm, log_target_hbm, log_source_hbm,
                 out_ref, kept_ref, peak_ref, bias_ref, target_norm_ref, source_norm_ref, log_target_ref,
                 log_source_ref, target_ref, source_ref, left_ref, right_ref, weight_ref, shift_ref, sems):
    cells, others = kept_ref.shape
    copies = arrive(
        [(source_hbm, source_ref), (log_target_hbm, log_target_ref), (target_hbm, target_ref),
         (log_source_hbm, log_source_ref)],
        sems,
    )
    copies[0].wait()
    fill_left(left_ref, source_ref)
    source_norm_ref[...] = jnp.broadcast_to(half_norms(source_ref[...]), source_norm_ref.shape)
    copies[1].wait()
    pot = log_target_ref[...] * LOG2E
    top = jnp.max(pot, axis=0, keepdims=True)
    weight_ref[...] = jnp.exp2(pot - top).astype(jnp.bfloat16)
    copies[2].wait()
    norms = half_norms(target_ref[...])
    target_norm_ref[...] = jnp.broadcast_to(norms, target_norm_ref.shape)
    bias = top - norms
    bias_ref[...] = jnp.broadcast_to(bias, bias_ref.shape)
    fill_right(right_ref, target_ref, bias)

    def scores(tile):
        best = None
        for at in range(0, others, CHUNK):
            part = slice(at, at + CHUNK)
            shift = jnp.dot(left_ref[tile * TILE : (tile + 1) * TILE, :], right_ref[:, part],
                            preferred_element_type=jnp.float32)
            shift_ref[tile % 2, :, part] = shift
            for k in range(0, CHUNK, LANES):
                best = shift[:, k : k + LANES] if best is None else jnp.maximum(best, shift[:, k : k + LANES])
        return jnp.max(best, axis=1, keepdims=True)

    tiles = cells // TILE
    peak = scores(0)
    for tile in range(tiles):
        rows = slice(tile * TILE, (tile + 1) * TILE)
        after = scores(tile + 1) if tile + 1 < tiles else None
        total = None
        for at in range(0, others, CHUNK):
            part = slice(at, at + CHUNK)
            kernel = jnp.exp2(shift_ref[tile % 2, :, part] - peak).astype(jnp.bfloat16)
            kept_ref[rows, part] = kernel
            sums = lax.dot_general(weight_ref[:, part], kernel, (((1,), (1,)), ((), ())),
                                   preferred_element_type=jnp.float32)
            total = sums if total is None else total + sums
        for k in range(TILE // LANES):
            part = slice(tile * TILE + k * LANES, tile * TILE + (k + 1) * LANES)
            row = jnp.broadcast_to(as_row(peak[k * LANES : (k + 1) * LANES]), (GROUP, LANES))
            peak_ref[:, part] = row
            result = jnp.log2(total[:, k * LANES : (k + 1) * LANES])
            for group in range(PAIRS // GROUP):
                place = tile_rows(group, tile * (TILE // LANES) + k, cells)
                out_ref[place, :] = row + result[group * GROUP : (group + 1) * GROUP]
        peak = after
    copies[3].wait()


def again(put, cells_ref, others_ref, log_ref, known_ref, pot_ref, left_ref, right_ref, weight_ref):
    cells, others = left_ref.shape[0], right_ref.shape[1]
    fill_left(left_ref, cells_ref)
    potentials(log_ref, known_ref, pot_ref)
    pot = pot_ref[...]
    top = jnp.max(pot, axis=0, keepdims=True)
    weight_ref[...] = jnp.exp2(pot - top).astype(jnp.bfloat16)
    fill_right(right_ref, others_ref, top)

    def tile(index, carry):
        rows = left_ref[pl.ds(pl.multiple_of(index * LANES, LANES), LANES), :]

        def chunk(step, carry):
            peak, total = carry
            part = pl.ds(pl.multiple_of(step * CHUNK, CHUNK), CHUNK)
            shift = jnp.dot(rows, right_ref[:, part], preferred_element_type=jnp.float32)
            best = jnp.maximum(peak, jnp.broadcast_to(jnp.max(shift, axis=1, keepdims=True), peak.shape))
            kernel = jnp.exp2(shift - best[:, :1]).astype(jnp.bfloat16)
            sums = lax.dot_general(weight_ref[:, part], kernel, (((1,), (1,)), ((), ())),
                                   preferred_element_type=jnp.float32)
            return best, total * jnp.exp2(peak - best).T[:1] + sums

        start = (jnp.full((LANES, LANES), -jnp.inf, jnp.float32), jnp.zeros((PAIRS, LANES), jnp.float32))
        peak, total = lax.fori_loop(0, others // CHUNK, chunk, start)
        put(index, peak.T[:1] + jnp.log2(total))
        return carry

    lax.fori_loop(0, cells // LANES, tile, 0)


def potentials(log_ref, known_ref, pot_ref, add=None):
    count = log_ref.shape[1]
    most = None
    for column in range(count // LANES):
        part = slice(column * LANES, (column + 1) * LANES)
        row = 0.0 if add is None else add(part)
        for group in range(PAIRS // GROUP):
            pairs = slice(group * GROUP, (group + 1) * GROUP)
            value = log_ref[pairs, part] * LOG2E - known_ref[tile_rows(group, column, count), :] + row
            pot_ref[pairs, part] = value
            most = value if most is None else jnp.maximum(most, value)
    return jnp.max(jnp.max(most, axis=0, keepdims=True), axis=1, keepdims=True)


def next_kernel(to_source, *refs):
    cells_hbm, others_hbm, log_ref, known_ref, kept_ref, peak_ref, bias_ref = refs[:7]
    outs = refs[7:8] if to_source else refs[7:9]
    cells_ref, others_ref, pot_ref, left_ref, right_ref, weight_ref, sems = refs[7 + len(outs) :]
    cells, others = left_ref.shape[0], right_ref.shape[1]
    groups = PAIRS // GROUP

    if to_source:
        most = potentials(log_ref, known_ref, pot_ref, lambda part: -bias_ref[:, part])

        def put(column, result):
            for group in range(groups):
                place = pl.ds((group * (cells // LANES) + column) * GROUP, GROUP)
                outs[0][place, :] = result[group * GROUP : (group + 1) * GROUP]
    else:
        most = potentials(log_ref, known_ref, pot_ref, lambda part: peak_ref[:, part])
        lower = lax.axis_index("core") == 0

        def put(column, result):
            for group in range(groups // 2):
                place = pl.ds((group * (cells // LANES) + column) * GROUP, GROUP)
                low = result[group * GROUP : (group + 1) * GROUP]
                high = result[(group + groups // 2) * GROUP : (group + groups // 2 + 1) * GROUP]
                outs[0][place, :] = jnp.where(lower, low, high)
                outs[1][place, :] = jnp.where(lower, high, low)

    weight_ref[...] = jnp.exp2(pot_ref[...] - most).astype(jnp.bfloat16)
    least = None
    for at in range(0, cells, TILE):
        if to_source:
            total = lax.dot_general(weight_ref[...], kept_ref[at : at + TILE, :], (((1,), (1,)), ((), ())),
                                    preferred_element_type=jnp.float32)
        else:
            total = jnp.dot(weight_ref[...], kept_ref[:, at : at + TILE], preferred_element_type=jnp.float32)
        least = total if least is None else jnp.minimum(least, total)
        for k in range(TILE // LANES):
            part = slice(at + k * LANES, at + (k + 1) * LANES)
            back = peak_ref[:1, part] if to_source else -bias_ref[:1, part]
            put(part.start // LANES, (back + most) + jnp.log2(total[:, k * LANES : (k + 1) * LANES]))
    least = jnp.min(least)

    @pl.when(jnp.logical_not(least >= SMALL))
    def _():
        for copy in arrive([(cells_hbm, cells_ref), (others_hbm, others_ref)], sems):
            copy.wait()
        again(put, cells_ref, others_ref, log_ref, known_ref, pot_ref, left_ref, right_ref, weight_ref)


LIMIT = pltpu.CompilerParams(vmem_limit_bytes=24 * 1024 * 1024)
HBM = pl.BlockSpec(memory_space=pltpu.HBM)
VMEM = pl.BlockSpec(memory_space=pltpu.VMEM)


def in_hbm(*arrays):
    return [pltpu.with_memory_space_constraint(array, pltpu.HBM) for array in arrays]


def first_update(target, source, log_target, log_source):
    others, cells = target.shape[1], source.shape[1]
    return pl.pallas_call(
        first_kernel,
        out_shape=[
            jax.ShapeDtypeStruct((PAIRS * cells // LANES, LANES), jnp.float32),
            jax.ShapeDtypeStruct((cells, others), jnp.bfloat16),
            jax.ShapeDtypeStruct((8, cells), jnp.float32),
            jax.ShapeDtypeStruct((8, others), jnp.float32),
            jax.ShapeDtypeStruct((8, others), jnp.float32),
            jax.ShapeDtypeStruct((8, cells), jnp.float32),
            jax.ShapeDtypeStruct(log_target.shape, log_target.dtype),
            jax.ShapeDtypeStruct(log_source.shape, log_source.dtype),
        ],
        in_specs=[HBM] * 4,
        out_specs=[VMEM] * 8,
        scratch_shapes=[
            pltpu.VMEM(target.shape, target.dtype),
            pltpu.VMEM(source.shape, source.dtype),
            pltpu.VMEM((cells, DEPTH), jnp.bfloat16),
            pltpu.VMEM((DEPTH, others), jnp.bfloat16),
            pltpu.VMEM((PAIRS, others), jnp.bfloat16),
            pltpu.VMEM((2, TILE, others), jnp.float32),
            pltpu.SemaphoreType.DMA((4,)),
        ],
        compiler_params=LIMIT,
    )(*in_hbm(target, source, log_target, log_source))


def next_update(cells, others, log, known, kept, to_source):
    own, count = cells.shape[1], others.shape[1]
    halves = 1 if to_source else 2
    return pl.pallas_call(
        functools.partial(next_kernel, to_source),
        out_shape=[jax.ShapeDtypeStruct((PAIRS * own // LANES // halves, LANES), jnp.float32)] * halves,
        in_specs=[HBM] * 2 + [VMEM] * (2 + len(kept)),
        out_specs=[VMEM] * halves,
        scratch_shapes=[
            pltpu.VMEM(cells.shape, cells.dtype),
            pltpu.VMEM(others.shape, others.dtype),
            pltpu.VMEM((PAIRS, count), jnp.float32),
            pltpu.VMEM((own, DEPTH), jnp.bfloat16),
            pltpu.VMEM((DEPTH, count), jnp.bfloat16),
            pltpu.VMEM((PAIRS, count), jnp.bfloat16),
            pltpu.SemaphoreType.DMA((2,)),
        ],
        compiler_params=LIMIT,
    )(*in_hbm(cells, others), log, known, *kept)


def log_sum(parts):
    best = jnp.max(parts, axis=0)
    return best + jnp.log2(jnp.sum(jnp.exp2(parts - best[None]), axis=0))


def combine_kernel(parts_ref, out_ref):
    out_ref[...] = jnp.broadcast_to(log_sum(parts_ref[...])[None], out_ref.shape)


def combine(parts, copies):
    return pl.pallas_call(
        combine_kernel,
        out_shape=jax.ShapeDtypeStruct((copies,) + parts.shape[1:], jnp.float32),
        compiler_params=pltpu.CompilerParams(vmem_limit_bytes=4 * 1024 * 1024),
    )(parts)


def join_kernel(mine_ref, others_ref, out_ref):
    mine = mine_ref[...]
    other = jnp.where(lax.axis_index("core") == 0, others_ref[1], others_ref[0])
    best = jnp.maximum(mine, other)
    out_ref[...] = best + jnp.log2(jnp.exp2(mine - best) + jnp.exp2(other - best))


def join(mine, others):
    return pl.pallas_call(
        join_kernel,
        out_shape=jax.ShapeDtypeStruct(mine.shape, jnp.float32),
        compiler_params=pltpu.CompilerParams(vmem_limit_bytes=4 * 1024 * 1024),
    )(mine, others)


def finish_kernel(*refs):
    inputs, outs, values, sems = refs[:4], refs[4:6], refs[6:8], refs[8]
    saves = []
    for side in range(2):
        known_ref, norm_ref = inputs[2 * side : 2 * side + 2]
        count = norm_ref.shape[1]
        for group in range(PAIRS // GROUP):
            pairs = slice(group * GROUP, (group + 1) * GROUP)
            for column in range(count // LANES):
                part = slice(column * LANES, (column + 1) * LANES)
                known = known_ref[tile_rows(group, column, count), :]
                values[side][pairs, part] = (known - norm_ref[:, part]) * BACK
            save = pltpu.make_async_copy(values[side].at[pairs], outs[side].at[pairs], sems.at[len(saves)])
            save.start()
            saves.append(save)
    for save in saves:
        save.wait()


def finish(source_known, source_norms, target_known, target_norms):
    shapes = [(PAIRS, norms.shape[1]) for norms in (source_norms, target_norms)]
    return pl.pallas_call(
        finish_kernel,
        out_shape=[jax.ShapeDtypeStruct(shape, jnp.float32) for shape in shapes],
        out_specs=[HBM] * 2,
        scratch_shapes=[pltpu.VMEM(shape, jnp.float32) for shape in shapes]
        + [pltpu.SemaphoreType.DMA((2 * PAIRS // GROUP,))],
        compiler_params=pltpu.CompilerParams(vmem_limit_bytes=4 * 1024 * 1024),
    )(source_known, source_norms, target_known, target_norms)


def count(sizes, axes):
    return math.prod(sizes[axis] for axis in axes)


def exchange(value, axes):
    return lax.all_to_all(value, axes, 0, 0)


def over_targets(parts, sizes):
    near, far = count(sizes, NEAR), count(sizes, FAR)
    rows = parts.shape[0]
    mine = exchange(parts.reshape(near, rows // near, LANES), NEAR)
    mine = exchange(combine(mine, far), FAR)
    return exchange(combine(mine, near), NEAR).reshape(rows, LANES)


def over_sources(mine, other, sizes):
    group = count(sizes, CHIPS)
    rows = mine.shape[0]
    mine = join(mine, lax.all_gather(other, "core"))
    mine = exchange(mine.reshape(group, rows // group, LANES), CHIPS)
    half = exchange(combine(mine, group), CHIPS).reshape(rows, LANES)
    return lax.all_gather(half, "core").reshape(2 * rows, LANES)


def body(sizes, source, target, log_source, log_target):
    source, target = source.T, target.T
    parts, *kept, target_norms, source_norms, log_target, log_source = first_update(
        target, source, log_target, log_source
    )
    for step in range(ITERS):
        if step:
            (parts,) = next_update(source, target, log_target, target_known, kept, True)
        source_known = over_targets(parts, sizes)
        target_known = over_sources(*next_update(target, source, log_source, source_known, kept, False), sizes)
    return finish(source_known, source_norms, target_known, target_norms)


def solution(mesh):
    sizes = {"yh": 2, "x": 4, "core": 2, "z3": 2, "z2": 2, "z1": 2, "z0": 2, "yl": 2}
    fine = Mesh(mesh.devices.reshape(tuple(sizes.values())), tuple(sizes))
    src, tgt = ("yh", "x", "core"), ("z3", "z2", "z1", "z0", "yl")
    in_specs = (P(src, None), P(tgt, None), P(None, src), P(None, tgt))
    out_specs = (P(None, src), P(None, tgt))
    return jax.shard_map(
        functools.partial(body, sizes), mesh=fine, in_specs=in_specs, out_specs=out_specs, check_vma=False
    )
```

```python
import functools
import math

import jax
import jax.numpy as jnp
from jax import lax
from jax.experimental import pallas as pl
from jax.experimental.pallas import tpu as pltpu
from jax.sharding import Mesh
from jax.sharding import PartitionSpec as P

FEAT = 64
ITERS = 2
PAIRS = 32
LANES = 128
GROUP = 8
DEPTH = 256

entropy = 0.1

LOG2E = math.log2(math.e)
HALF = LOG2E / (FEAT * entropy)
SCALE = 2.0 * HALF
BACK = -entropy / LOG2E
HIGH = 24.0
SMALL = 2.0**-66

NEAR = ("z0", "yl", "z1")
FAR = ("z2", "z3")
CHIPS = ("x", "yh")

TILE = 256
CHUNK = 512


def pieces(value):
    high = value.astype(jnp.bfloat16)
    rest = value - high.astype(jnp.float32)
    middle = rest.astype(jnp.bfloat16)
    low = (rest - middle.astype(jnp.float32)).astype(jnp.bfloat16)
    return (high, middle, low)


def half_norms(feats):
    return jnp.sum(jnp.square(feats.astype(jnp.float32)), axis=0, keepdims=True) * HALF


def fill_left(left_ref, cells_ref):
    for at in range(0, left_ref.shape[0], LANES):
        part = slice(at, at + LANES)
        scaled = cells_ref[:, part].astype(jnp.float32) * SCALE
        row = lax.broadcasted_iota(jnp.int32, (LANES - FEAT, LANES), 0)
        ones = jnp.where(row < 3, 1.0, 0.0)
        high, middle, low = (x.astype(jnp.float32) for x in pieces(scaled))
        left_ref[part, :LANES] = jnp.concatenate([high, middle], axis=0).T.astype(jnp.bfloat16)
        left_ref[part, LANES:] = jnp.concatenate([low, ones], axis=0).T.astype(jnp.bfloat16)


def fill_right(right_ref, others_ref, bias):
    count = others_ref.shape[1]
    feats = others_ref[...]
    for k in range(3):
        right_ref[k * FEAT : (k + 1) * FEAT, :] = feats
    row = lax.broadcasted_iota(jnp.int32, (16, count), 0)
    high, middle, low = (jnp.broadcast_to(x.astype(jnp.float32), (16, count)) for x in pieces(bias))
    block = jnp.where(row == 0, high, jnp.where(row == 1, middle, jnp.where(row == 2, low, 0.0)))
    right_ref[3 * FEAT : 3 * FEAT + 16, :] = block.astype(jnp.bfloat16)
    right_ref[3 * FEAT + 16 :, :] = jnp.zeros((DEPTH - 3 * FEAT - 16, count), jnp.bfloat16)


def tile_rows(group, column, count):
    return slice((group * (count // LANES) + column) * GROUP, (group * (count // LANES) + column + 1) * GROUP)


def as_row(column):
    rows = column.shape[0]
    return jnp.broadcast_to(column, (rows, LANES)).T[:1]


def arrive(pairs, sems):
    copies = [pltpu.make_async_copy(src, dst, sems.at[k]) for k, (src, dst) in enumerate(pairs)]
    for copy in copies:
        copy.start()
    return copies


def first_kernel(target_hbm, source_hbm, log_target_hbm, log_source_hbm,
                 out_ref, kept_ref, peak_ref, bias_ref, target_norm_ref, source_norm_ref, log_target_ref,
                 log_source_ref, target_ref, source_ref, left_ref, right_ref, weight_ref, shift_ref, sems):
    cells, others = kept_ref.shape
    copies = arrive(
        [(source_hbm, source_ref), (log_target_hbm, log_target_ref), (target_hbm, target_ref),
         (log_source_hbm, log_source_ref)],
        sems,
    )
    copies[0].wait()
    fill_left(left_ref, source_ref)
    source_norm_ref[...] = jnp.broadcast_to(half_norms(source_ref[...]), source_norm_ref.shape)
    copies[1].wait()
    pot = log_target_ref[...] * LOG2E
    top = jnp.max(pot, axis=0, keepdims=True)
    weight_ref[...] = jnp.exp2(pot - top).astype(jnp.bfloat16)
    copies[2].wait()
    norms = half_norms(target_ref[...])
    target_norm_ref[...] = jnp.broadcast_to(norms, target_norm_ref.shape)
    bias = top - norms
    bias_ref[...] = jnp.broadcast_to(bias, bias_ref.shape)
    fill_right(right_ref, target_ref, bias)

    def scores(tile):
        best = None
        for at in range(0, others, CHUNK):
            part = slice(at, at + CHUNK)
            shift = jnp.dot(left_ref[tile * TILE : (tile + 1) * TILE, :], right_ref[:, part],
                            preferred_element_type=jnp.float32)
            shift_ref[tile % 2, :, part] = shift
            for k in range(0, CHUNK, LANES):
                best = shift[:, k : k + LANES] if best is None else jnp.maximum(best, shift[:, k : k + LANES])
        return jnp.max(best, axis=1, keepdims=True)

    tiles = cells // TILE
    peak = scores(0)
    for tile in range(tiles):
        rows = slice(tile * TILE, (tile + 1) * TILE)
        after = scores(tile + 1) if tile + 1 < tiles else None
        total = None
        for at in range(0, others, CHUNK):
            part = slice(at, at + CHUNK)
            kernel = jnp.exp2(shift_ref[tile % 2, :, part] - peak).astype(jnp.bfloat16)
            kept_ref[rows, part] = kernel
            sums = lax.dot_general(weight_ref[:, part], kernel, (((1,), (1,)), ((), ())),
                                   preferred_element_type=jnp.float32)
            total = sums if total is None else total + sums
        for k in range(TILE // LANES):
            part = slice(tile * TILE + k * LANES, tile * TILE + (k + 1) * LANES)
            row = jnp.broadcast_to(as_row(peak[k * LANES : (k + 1) * LANES]), (GROUP, LANES))
            peak_ref[:, part] = row
            result = jnp.log2(total[:, k * LANES : (k + 1) * LANES])
            for group in range(PAIRS // GROUP):
                place = tile_rows(group, tile * (TILE // LANES) + k, cells)
                out_ref[place, :] = row + result[group * GROUP : (group + 1) * GROUP]
        peak = after
    copies[3].wait()


def again(put, cells_ref, others_ref, log_ref, known_ref, pot_ref, left_ref, right_ref, weight_ref):
    cells, others = left_ref.shape[0], right_ref.shape[1]
    fill_left(left_ref, cells_ref)
    potentials(log_ref, known_ref, pot_ref)
    pot = pot_ref[...]
    top = jnp.max(pot, axis=0, keepdims=True)
    weight_ref[...] = jnp.exp2(pot - top).astype(jnp.bfloat16)
    fill_right(right_ref, others_ref, top)

    def tile(index, carry):
        rows = left_ref[pl.ds(pl.multiple_of(index * LANES, LANES), LANES), :]

        def chunk(step, carry):
            peak, total = carry
            part = pl.ds(pl.multiple_of(step * CHUNK, CHUNK), CHUNK)
            shift = jnp.dot(rows, right_ref[:, part], preferred_element_type=jnp.float32)
            best = jnp.maximum(peak, jnp.broadcast_to(jnp.max(shift, axis=1, keepdims=True), peak.shape))
            kernel = jnp.exp2(shift - best[:, :1]).astype(jnp.bfloat16)
            sums = lax.dot_general(weight_ref[:, part], kernel, (((1,), (1,)), ((), ())),
                                   preferred_element_type=jnp.float32)
            return best, total * jnp.exp2(peak - best).T[:1] + sums

        start = (jnp.full((LANES, LANES), -jnp.inf, jnp.float32), jnp.zeros((PAIRS, LANES), jnp.float32))
        peak, total = lax.fori_loop(0, others // CHUNK, chunk, start)
        put(index, peak.T[:1] + jnp.log2(total))
        return carry

    lax.fori_loop(0, cells // LANES, tile, 0)


def potentials(log_ref, known_ref, pot_ref):
    count = log_ref.shape[1]
    for column in range(count // LANES):
        part = slice(column * LANES, (column + 1) * LANES)
        for group in range(PAIRS // GROUP):
            pairs = slice(group * GROUP, (group + 1) * GROUP)
            pot_ref[pairs, part] = log_ref[pairs, part] * LOG2E - known_ref[tile_rows(group, column, count), :]


def rescaled(log_ref, known_ref, weight_ref, add):
    count = log_ref.shape[1]
    most = None
    for column in range(count // LANES):
        part = slice(column * LANES, (column + 1) * LANES)
        row = add(part)
        for group in range(0, PAIRS // GROUP, 2):
            two = []
            for one in (group, group + 1):
                logs = log_ref[one * GROUP : (one + 1) * GROUP, part]
                value = logs * LOG2E - known_ref[tile_rows(one, column, count), :] + row
                most = value if most is None else jnp.maximum(most, value)
                two.append(jnp.exp2(value))
            both = jnp.concatenate(two, axis=0).astype(jnp.bfloat16)
            weight_ref[group * GROUP : (group + 2) * GROUP, part] = both
    return most


def next_kernel(to_source, *refs):
    cells_hbm, others_hbm, log_ref, known_ref, kept_ref, peak_ref, bias_ref = refs[:7]
    outs = refs[7:8] if to_source else refs[7:9]
    cells_ref, others_ref, pot_ref, left_ref, right_ref, weight_ref, sems = refs[7 + len(outs) :]
    cells, others = left_ref.shape[0], right_ref.shape[1]
    groups = PAIRS // GROUP

    if to_source:
        most = rescaled(log_ref, known_ref, weight_ref, lambda part: -bias_ref[:, part])

        def put(column, result):
            for group in range(groups):
                place = pl.ds((group * (cells // LANES) + column) * GROUP, GROUP)
                outs[0][place, :] = result[group * GROUP : (group + 1) * GROUP]
    else:
        most = rescaled(log_ref, known_ref, weight_ref, lambda part: peak_ref[:, part])
        lower = lax.axis_index("core") == 0

        def put(column, result):
            for group in range(groups // 2):
                place = pl.ds((group * (cells // LANES) + column) * GROUP, GROUP)
                low = result[group * GROUP : (group + 1) * GROUP]
                high = result[(group + groups // 2) * GROUP : (group + groups // 2 + 1) * GROUP]
                outs[0][place, :] = jnp.where(lower, low, high)
                outs[1][place, :] = jnp.where(lower, high, low)

    least = None
    for at in range(0, cells, TILE):
        if to_source:
            total = lax.dot_general(weight_ref[...], kept_ref[at : at + TILE, :], (((1,), (1,)), ((), ())),
                                    preferred_element_type=jnp.float32)
        else:
            total = jnp.dot(weight_ref[...], kept_ref[:, at : at + TILE], preferred_element_type=jnp.float32)
        least = total if least is None else jnp.minimum(least, total)
        for k in range(TILE // LANES):
            part = slice(at + k * LANES, at + (k + 1) * LANES)
            back = peak_ref[:1, part] if to_source else -bias_ref[:1, part]
            put(part.start // LANES, back + jnp.log2(total[:, k * LANES : (k + 1) * LANES]))
    fits = jnp.logical_and(jnp.min(least) >= SMALL, jnp.max(most) <= HIGH)

    @pl.when(jnp.logical_not(fits))
    def _():
        for copy in arrive([(cells_hbm, cells_ref), (others_hbm, others_ref)], sems):
            copy.wait()
        again(put, cells_ref, others_ref, log_ref, known_ref, pot_ref, left_ref, right_ref, weight_ref)


LIMIT = pltpu.CompilerParams(vmem_limit_bytes=24 * 1024 * 1024)
HBM = pl.BlockSpec(memory_space=pltpu.HBM)
VMEM = pl.BlockSpec(memory_space=pltpu.VMEM)


def in_hbm(*arrays):
    return [pltpu.with_memory_space_constraint(array, pltpu.HBM) for array in arrays]


def first_update(target, source, log_target, log_source):
    others, cells = target.shape[1], source.shape[1]
    return pl.pallas_call(
        first_kernel,
        out_shape=[
            jax.ShapeDtypeStruct((PAIRS * cells // LANES, LANES), jnp.float32),
            jax.ShapeDtypeStruct((cells, others), jnp.bfloat16),
            jax.ShapeDtypeStruct((8, cells), jnp.float32),
            jax.ShapeDtypeStruct((8, others), jnp.float32),
            jax.ShapeDtypeStruct((8, others), jnp.float32),
            jax.ShapeDtypeStruct((8, cells), jnp.float32),
            jax.ShapeDtypeStruct(log_target.shape, log_target.dtype),
            jax.ShapeDtypeStruct(log_source.shape, log_source.dtype),
        ],
        in_specs=[HBM] * 4,
        out_specs=[VMEM] * 8,
        scratch_shapes=[
            pltpu.VMEM(target.shape, target.dtype),
            pltpu.VMEM(source.shape, source.dtype),
            pltpu.VMEM((cells, DEPTH), jnp.bfloat16),
            pltpu.VMEM((DEPTH, others), jnp.bfloat16),
            pltpu.VMEM((PAIRS, others), jnp.bfloat16),
            pltpu.VMEM((2, TILE, others), jnp.float32),
            pltpu.SemaphoreType.DMA((4,)),
        ],
        compiler_params=LIMIT,
    )(*in_hbm(target, source, log_target, log_source))


def next_update(cells, others, log, known, kept, to_source):
    own, count = cells.shape[1], others.shape[1]
    halves = 1 if to_source else 2
    return pl.pallas_call(
        functools.partial(next_kernel, to_source),
        out_shape=[jax.ShapeDtypeStruct((PAIRS * own // LANES // halves, LANES), jnp.float32)] * halves,
        in_specs=[HBM] * 2 + [VMEM] * (2 + len(kept)),
        out_specs=[VMEM] * halves,
        scratch_shapes=[
            pltpu.VMEM(cells.shape, cells.dtype),
            pltpu.VMEM(others.shape, others.dtype),
            pltpu.VMEM((PAIRS, count), jnp.float32),
            pltpu.VMEM((own, DEPTH), jnp.bfloat16),
            pltpu.VMEM((DEPTH, count), jnp.bfloat16),
            pltpu.VMEM((PAIRS, count), jnp.bfloat16),
            pltpu.SemaphoreType.DMA((2,)),
        ],
        compiler_params=LIMIT,
    )(*in_hbm(cells, others), log, known, *kept)


def log_sum(parts):
    best = jnp.max(parts, axis=0)
    return best + jnp.log2(jnp.sum(jnp.exp2(parts - best[None]), axis=0))


def combine_kernel(parts_ref, out_ref):
    out_ref[...] = jnp.broadcast_to(log_sum(parts_ref[...])[None], out_ref.shape)


def combine(parts, copies):
    return pl.pallas_call(
        combine_kernel,
        out_shape=jax.ShapeDtypeStruct((copies,) + parts.shape[1:], jnp.float32),
        compiler_params=pltpu.CompilerParams(vmem_limit_bytes=4 * 1024 * 1024),
    )(parts)


def join_kernel(mine_ref, others_ref, out_ref):
    mine = mine_ref[...]
    other = jnp.where(lax.axis_index("core") == 0, others_ref[1], others_ref[0])
    best = jnp.maximum(mine, other)
    out_ref[...] = best + jnp.log2(jnp.exp2(mine - best) + jnp.exp2(other - best))


def join(mine, others):
    return pl.pallas_call(
        join_kernel,
        out_shape=jax.ShapeDtypeStruct(mine.shape, jnp.float32),
        compiler_params=pltpu.CompilerParams(vmem_limit_bytes=4 * 1024 * 1024),
    )(mine, others)


def finish_kernel(*refs):
    inputs, outs, values, sems = refs[:4], refs[4:6], refs[6:8], refs[8]
    saves = []
    for side in range(2):
        known_ref, norm_ref = inputs[2 * side : 2 * side + 2]
        count = norm_ref.shape[1]
        for group in range(PAIRS // GROUP):
            pairs = slice(group * GROUP, (group + 1) * GROUP)
            for column in range(count // LANES):
                part = slice(column * LANES, (column + 1) * LANES)
                known = known_ref[tile_rows(group, column, count), :]
                values[side][pairs, part] = (known - norm_ref[:, part]) * BACK
            save = pltpu.make_async_copy(values[side].at[pairs], outs[side].at[pairs], sems.at[len(saves)])
            save.start()
            saves.append(save)
    for save in saves:
        save.wait()


def finish(source_known, source_norms, target_known, target_norms):
    shapes = [(PAIRS, norms.shape[1]) for norms in (source_norms, target_norms)]
    return pl.pallas_call(
        finish_kernel,
        out_shape=[jax.ShapeDtypeStruct(shape, jnp.float32) for shape in shapes],
        out_specs=[HBM] * 2,
        scratch_shapes=[pltpu.VMEM(shape, jnp.float32) for shape in shapes]
        + [pltpu.SemaphoreType.DMA((2 * PAIRS // GROUP,))],
        compiler_params=pltpu.CompilerParams(vmem_limit_bytes=4 * 1024 * 1024),
    )(source_known, source_norms, target_known, target_norms)


def count(sizes, axes):
    return math.prod(sizes[axis] for axis in axes)


def exchange(value, axes):
    return lax.all_to_all(value, axes, 0, 0)


def over_targets(parts, sizes):
    near, far = count(sizes, NEAR), count(sizes, FAR)
    rows = parts.shape[0]
    mine = exchange(parts.reshape(near, rows // near, LANES), NEAR)
    mine = exchange(combine(mine, far), FAR)
    return exchange(combine(mine, near), NEAR).reshape(rows, LANES)


def over_sources(mine, other, sizes):
    group = count(sizes, CHIPS)
    rows = mine.shape[0]
    mine = join(mine, lax.all_gather(other, "core"))
    mine = exchange(mine.reshape(group, rows // group, LANES), CHIPS)
    half = exchange(combine(mine, group), CHIPS).reshape(rows, LANES)
    return lax.all_gather(half, "core").reshape(2 * rows, LANES)


def body(sizes, source, target, log_source, log_target):
    source, target = source.T, target.T
    parts, *kept, target_norms, source_norms, log_target, log_source = first_update(
        target, source, log_target, log_source
    )
    for step in range(ITERS):
        if step:
            (parts,) = next_update(source, target, log_target, target_known, kept, True)
        source_known = over_targets(parts, sizes)
        target_known = over_sources(*next_update(target, source, log_source, source_known, kept, False), sizes)
    return finish(source_known, source_norms, target_known, target_norms)


def solution(mesh):
    sizes = {"yh": 2, "x": 4, "core": 2, "z3": 2, "z2": 2, "z1": 2, "z0": 2, "yl": 2}
    fine = Mesh(mesh.devices.reshape(tuple(sizes.values())), tuple(sizes))
    src, tgt = ("yh", "x", "core"), ("z3", "z2", "z1", "z0", "yl")
    in_specs = (P(src, None), P(tgt, None), P(None, src), P(None, tgt))
    out_specs = (P(None, src), P(None, tgt))
    return jax.shard_map(
        functools.partial(body, sizes), mesh=fine, in_specs=in_specs, out_specs=out_specs, check_vma=False
    )
```

```python
import functools
import math

import jax
import jax.numpy as jnp
from jax import lax
from jax.experimental import pallas as pl
from jax.experimental.pallas import tpu as pltpu
from jax.sharding import Mesh
from jax.sharding import PartitionSpec as P

FEAT = 64
ITERS = 2
PAIRS = 32
LANES = 128
GROUP = 8
DEPTH = 256

entropy = 0.1

LOG2E = math.log2(math.e)
HALF = LOG2E / (FEAT * entropy)
SCALE = 2.0 * HALF
BACK = -entropy / LOG2E
HIGH = 24.0
SMALL = 2.0**-66

NEAR = ("z0", "yl", "z1")
FAR = ("z2", "z3")
CHIPS = ("x", "yh")

TILE = 256
CHUNK = 512


def pieces(value):
    high = value.astype(jnp.bfloat16)
    rest = value - high.astype(jnp.float32)
    middle = rest.astype(jnp.bfloat16)
    low = (rest - middle.astype(jnp.float32)).astype(jnp.bfloat16)
    return (high, middle, low)


def half_norms(feats):
    return jnp.sum(jnp.square(feats.astype(jnp.float32)), axis=0, keepdims=True) * HALF


def fill_left(left_ref, cells_ref):
    for at in range(0, left_ref.shape[0], LANES):
        part = slice(at, at + LANES)
        scaled = cells_ref[:, part].astype(jnp.float32) * SCALE
        row = lax.broadcasted_iota(jnp.int32, (LANES - FEAT, LANES), 0)
        ones = jnp.where(row < 3, 1.0, 0.0)
        high, middle, low = (x.astype(jnp.float32) for x in pieces(scaled))
        left_ref[part, :LANES] = jnp.concatenate([high, middle], axis=0).T.astype(jnp.bfloat16)
        left_ref[part, LANES:] = jnp.concatenate([low, ones], axis=0).T.astype(jnp.bfloat16)


def fill_right(right_ref, others_ref, bias):
    count = others_ref.shape[1]
    feats = others_ref[...]
    for k in range(3):
        right_ref[k * FEAT : (k + 1) * FEAT, :] = feats
    row = lax.broadcasted_iota(jnp.int32, (16, count), 0)
    high, middle, low = (jnp.broadcast_to(x.astype(jnp.float32), (16, count)) for x in pieces(bias))
    block = jnp.where(row == 0, high, jnp.where(row == 1, middle, jnp.where(row == 2, low, 0.0)))
    right_ref[3 * FEAT : 3 * FEAT + 16, :] = block.astype(jnp.bfloat16)
    right_ref[3 * FEAT + 16 :, :] = jnp.zeros((DEPTH - 3 * FEAT - 16, count), jnp.bfloat16)


def tile_rows(group, column, count):
    return slice((group * (count // LANES) + column) * GROUP, (group * (count // LANES) + column + 1) * GROUP)


def as_row(column):
    rows = column.shape[0]
    return jnp.broadcast_to(column, (rows, LANES)).T[:1]


def arrive(pairs, sems):
    copies = [pltpu.make_async_copy(src, dst, sems.at[k]) for k, (src, dst) in enumerate(pairs)]
    for copy in copies:
        copy.start()
    return copies


def first_kernel(target_hbm, source_hbm, log_target_hbm, log_source_hbm,
                 out_ref, kept_ref, peak_ref, bias_ref, target_norm_ref, source_norm_ref, log_target_ref,
                 log_source_ref, target_ref, source_ref, left_ref, right_ref, weight_ref, shift_ref, sems):
    cells, others = kept_ref.shape
    copies = arrive(
        [(source_hbm, source_ref), (log_target_hbm, log_target_ref), (target_hbm, target_ref),
         (log_source_hbm, log_source_ref)],
        sems,
    )
    copies[0].wait()
    fill_left(left_ref, source_ref)
    source_norm_ref[...] = jnp.broadcast_to(half_norms(source_ref[...]), source_norm_ref.shape)
    copies[1].wait()
    pot = log_target_ref[...] * LOG2E
    top = jnp.max(pot, axis=0, keepdims=True)
    weight_ref[...] = jnp.exp2(pot - top).astype(jnp.bfloat16)
    copies[2].wait()
    norms = half_norms(target_ref[...])
    target_norm_ref[...] = jnp.broadcast_to(norms, target_norm_ref.shape)
    bias = top - norms
    bias_ref[...] = jnp.broadcast_to(bias, bias_ref.shape)
    fill_right(right_ref, target_ref, bias)

    def scores(tile):
        best = None
        for at in range(0, others, CHUNK):
            part = slice(at, at + CHUNK)
            shift = jnp.dot(left_ref[tile * TILE : (tile + 1) * TILE, :], right_ref[:, part],
                            preferred_element_type=jnp.float32)
            shift_ref[tile % 2, :, part] = shift
            for k in range(0, CHUNK, LANES):
                best = shift[:, k : k + LANES] if best is None else jnp.maximum(best, shift[:, k : k + LANES])
        return jnp.max(best, axis=1, keepdims=True)

    tiles = cells // TILE
    peak = scores(0)
    for tile in range(tiles):
        rows = slice(tile * TILE, (tile + 1) * TILE)
        after = scores(tile + 1) if tile + 1 < tiles else None
        total = None
        for at in range(0, others, CHUNK):
            part = slice(at, at + CHUNK)
            kernel = jnp.exp2(shift_ref[tile % 2, :, part] - peak).astype(jnp.bfloat16)
            kept_ref[rows, part] = kernel
            sums = lax.dot_general(weight_ref[:, part], kernel, (((1,), (1,)), ((), ())),
                                   preferred_element_type=jnp.float32)
            total = sums if total is None else total + sums
        for k in range(TILE // LANES):
            part = slice(tile * TILE + k * LANES, tile * TILE + (k + 1) * LANES)
            row = jnp.broadcast_to(as_row(peak[k * LANES : (k + 1) * LANES]), (GROUP, LANES))
            peak_ref[:, part] = row
            result = jnp.log2(total[:, k * LANES : (k + 1) * LANES])
            for group in range(PAIRS // GROUP):
                place = tile_rows(group, tile * (TILE // LANES) + k, cells)
                out_ref[place, :] = row + result[group * GROUP : (group + 1) * GROUP]
        peak = after
    copies[3].wait()


def again(put, cells_ref, others_ref, log_ref, known_ref, pot_ref, left_ref, right_ref, weight_ref):
    cells, others = left_ref.shape[0], right_ref.shape[1]
    fill_left(left_ref, cells_ref)
    potentials(log_ref, known_ref, pot_ref)
    pot = pot_ref[...]
    top = jnp.max(pot, axis=0, keepdims=True)
    weight_ref[...] = jnp.exp2(pot - top).astype(jnp.bfloat16)
    fill_right(right_ref, others_ref, top)

    def tile(index, carry):
        rows = left_ref[pl.ds(pl.multiple_of(index * LANES, LANES), LANES), :]

        def chunk(step, carry):
            peak, total = carry
            part = pl.ds(pl.multiple_of(step * CHUNK, CHUNK), CHUNK)
            shift = jnp.dot(rows, right_ref[:, part], preferred_element_type=jnp.float32)
            best = jnp.maximum(peak, jnp.broadcast_to(jnp.max(shift, axis=1, keepdims=True), peak.shape))
            kernel = jnp.exp2(shift - best[:, :1]).astype(jnp.bfloat16)
            sums = lax.dot_general(weight_ref[:, part], kernel, (((1,), (1,)), ((), ())),
                                   preferred_element_type=jnp.float32)
            return best, total * jnp.exp2(peak - best).T[:1] + sums

        start = (jnp.full((LANES, LANES), -jnp.inf, jnp.float32), jnp.zeros((PAIRS, LANES), jnp.float32))
        peak, total = lax.fori_loop(0, others // CHUNK, chunk, start)
        put(index, peak.T[:1] + jnp.log2(total))
        return carry

    lax.fori_loop(0, cells // LANES, tile, 0)


def potentials(log_ref, known_ref, pot_ref):
    count = log_ref.shape[1]
    for column in range(count // LANES):
        part = slice(column * LANES, (column + 1) * LANES)
        for group in range(PAIRS // GROUP):
            pairs = slice(group * GROUP, (group + 1) * GROUP)
            pot_ref[pairs, part] = log_ref[pairs, part] * LOG2E - known_ref[tile_rows(group, column, count), :]


def rescaled(log_ref, known_ref, weight_ref, add):
    count = log_ref.shape[1]
    most = None
    for column in range(count // LANES):
        part = slice(column * LANES, (column + 1) * LANES)
        row = add(part)
        for group in range(0, PAIRS // GROUP, 2):
            two = []
            for one in (group, group + 1):
                logs = log_ref[one * GROUP : (one + 1) * GROUP, part]
                value = logs * LOG2E - known_ref[tile_rows(one, column, count), :] + row
                most = value if most is None else jnp.maximum(most, value)
                two.append(jnp.exp2(value))
            both = jnp.concatenate(two, axis=0).astype(jnp.bfloat16)
            weight_ref[group * GROUP : (group + 2) * GROUP, part] = both
    return most


def next_kernel(to_source, *refs):
    cells_hbm, others_hbm, log_ref, known_ref, kept_ref, peak_ref, bias_ref = refs[:7]
    outs = refs[7:8] if to_source else refs[7:9]
    cells_ref, others_ref, pot_ref, left_ref, right_ref, weight_ref, sems = refs[7 + len(outs) :]
    cells, others = left_ref.shape[0], right_ref.shape[1]
    groups = PAIRS // GROUP

    if to_source:
        most = rescaled(log_ref, known_ref, weight_ref, lambda part: -bias_ref[:, part])

        def put(column, result):
            for group in range(groups):
                place = pl.ds((group * (cells // LANES) + column) * GROUP, GROUP)
                outs[0][place, :] = result[group * GROUP : (group + 1) * GROUP]
    else:
        most = rescaled(log_ref, known_ref, weight_ref, lambda part: peak_ref[:, part])
        lower = lax.axis_index("core") == 0

        def put(column, result):
            for group in range(groups // 2):
                place = pl.ds((group * (cells // LANES) + column) * GROUP, GROUP)
                low = result[group * GROUP : (group + 1) * GROUP]
                high = result[(group + groups // 2) * GROUP : (group + groups // 2 + 1) * GROUP]
                outs[0][place, :] = jnp.where(lower, low, high)
                outs[1][place, :] = jnp.where(lower, high, low)

    least = None
    for at in range(0, cells, TILE):
        if to_source:
            total = lax.dot_general(weight_ref[...], kept_ref[at : at + TILE, :], (((1,), (1,)), ((), ())),
                                    preferred_element_type=jnp.float32)
        else:
            total = jnp.dot(weight_ref[...], kept_ref[:, at : at + TILE], preferred_element_type=jnp.float32)
        least = total if least is None else jnp.minimum(least, total)
        for k in range(TILE // LANES):
            part = slice(at + k * LANES, at + (k + 1) * LANES)
            back = peak_ref[:1, part] if to_source else -bias_ref[:1, part]
            put(part.start // LANES, back + jnp.log2(total[:, k * LANES : (k + 1) * LANES]))
    fits = jnp.logical_and(jnp.min(least) >= SMALL, jnp.max(most) <= HIGH)

    @pl.when(jnp.logical_not(fits))
    def _():
        for copy in arrive([(cells_hbm, cells_ref), (others_hbm, others_ref)], sems):
            copy.wait()
        again(put, cells_ref, others_ref, log_ref, known_ref, pot_ref, left_ref, right_ref, weight_ref)


LIMIT = pltpu.CompilerParams(vmem_limit_bytes=24 * 1024 * 1024)
HBM = pl.BlockSpec(memory_space=pltpu.HBM)
VMEM = pl.BlockSpec(memory_space=pltpu.VMEM)


def in_hbm(*arrays):
    return [pltpu.with_memory_space_constraint(array, pltpu.HBM) for array in arrays]


def first_update(target, source, log_target, log_source):
    others, cells = target.shape[1], source.shape[1]
    return pl.pallas_call(
        first_kernel,
        out_shape=[
            jax.ShapeDtypeStruct((PAIRS * cells // LANES, LANES), jnp.float32),
            jax.ShapeDtypeStruct((cells, others), jnp.bfloat16),
            jax.ShapeDtypeStruct((8, cells), jnp.float32),
            jax.ShapeDtypeStruct((8, others), jnp.float32),
            jax.ShapeDtypeStruct((8, others), jnp.float32),
            jax.ShapeDtypeStruct((8, cells), jnp.float32),
            jax.ShapeDtypeStruct(log_target.shape, log_target.dtype),
            jax.ShapeDtypeStruct(log_source.shape, log_source.dtype),
        ],
        in_specs=[HBM] * 4,
        out_specs=[VMEM] * 8,
        scratch_shapes=[
            pltpu.VMEM(target.shape, target.dtype),
            pltpu.VMEM(source.shape, source.dtype),
            pltpu.VMEM((cells, DEPTH), jnp.bfloat16),
            pltpu.VMEM((DEPTH, others), jnp.bfloat16),
            pltpu.VMEM((PAIRS, others), jnp.bfloat16),
            pltpu.VMEM((2, TILE, others), jnp.float32),
            pltpu.SemaphoreType.DMA((4,)),
        ],
        compiler_params=LIMIT,
    )(*in_hbm(target, source, log_target, log_source))


def next_update(cells, others, log, known, kept, to_source):
    own, count = cells.shape[1], others.shape[1]
    halves = 1 if to_source else 2
    return pl.pallas_call(
        functools.partial(next_kernel, to_source),
        out_shape=[jax.ShapeDtypeStruct((PAIRS * own // LANES // halves, LANES), jnp.float32)] * halves,
        in_specs=[HBM] * 2 + [VMEM] * (2 + len(kept)),
        out_specs=[VMEM] * halves,
        scratch_shapes=[
            pltpu.VMEM(cells.shape, cells.dtype),
            pltpu.VMEM(others.shape, others.dtype),
            pltpu.VMEM((PAIRS, count), jnp.float32),
            pltpu.VMEM((own, DEPTH), jnp.bfloat16),
            pltpu.VMEM((DEPTH, count), jnp.bfloat16),
            pltpu.VMEM((PAIRS, count), jnp.bfloat16),
            pltpu.SemaphoreType.DMA((2,)),
        ],
        compiler_params=LIMIT,
    )(*in_hbm(cells, others), log, known, *kept)


def log_sum(parts):
    best = jnp.max(parts, axis=0)
    return best + jnp.log2(jnp.sum(jnp.exp2(parts - best[None]), axis=0))


def combine_kernel(parts_ref, out_ref):
    out_ref[...] = jnp.broadcast_to(log_sum(parts_ref[...])[None], out_ref.shape)


def combine(parts, copies):
    return pl.pallas_call(
        combine_kernel,
        out_shape=jax.ShapeDtypeStruct((copies,) + parts.shape[1:], jnp.float32),
        compiler_params=pltpu.CompilerParams(vmem_limit_bytes=4 * 1024 * 1024),
    )(parts)


def join_kernel(mine_ref, others_ref, out_ref):
    mine = mine_ref[...]
    other = others_ref[1 - lax.axis_index("core")]
    best = jnp.maximum(mine, other)
    out_ref[...] = best + jnp.log2(jnp.exp2(mine - best) + jnp.exp2(other - best))


def join(mine, others):
    return pl.pallas_call(
        join_kernel,
        out_shape=jax.ShapeDtypeStruct(mine.shape, jnp.float32),
        compiler_params=pltpu.CompilerParams(vmem_limit_bytes=4 * 1024 * 1024),
    )(mine, others)


def finish_kernel(*refs):
    inputs, outs, values, sems = refs[:4], refs[4:6], refs[6:8], refs[8]
    saves = []
    for side in range(2):
        known_ref, norm_ref = inputs[2 * side : 2 * side + 2]
        count = norm_ref.shape[1]
        for group in range(PAIRS // GROUP):
            pairs = slice(group * GROUP, (group + 1) * GROUP)
            for column in range(count // LANES):
                part = slice(column * LANES, (column + 1) * LANES)
                known = known_ref[tile_rows(group, column, count), :]
                values[side][pairs, part] = (known - norm_ref[:, part]) * BACK
            save = pltpu.make_async_copy(values[side].at[pairs], outs[side].at[pairs], sems.at[len(saves)])
            save.start()
            saves.append(save)
    for save in saves:
        save.wait()


def finish(source_known, source_norms, target_known, target_norms):
    shapes = [(PAIRS, norms.shape[1]) for norms in (source_norms, target_norms)]
    return pl.pallas_call(
        finish_kernel,
        out_shape=[jax.ShapeDtypeStruct(shape, jnp.float32) for shape in shapes],
        out_specs=[HBM] * 2,
        scratch_shapes=[pltpu.VMEM(shape, jnp.float32) for shape in shapes]
        + [pltpu.SemaphoreType.DMA((2 * PAIRS // GROUP,))],
        compiler_params=pltpu.CompilerParams(vmem_limit_bytes=4 * 1024 * 1024),
    )(source_known, source_norms, target_known, target_norms)


def count(sizes, axes):
    return math.prod(sizes[axis] for axis in axes)


def exchange(value, axes):
    return lax.all_to_all(value, axes, 0, 0)


def over_targets(parts, sizes):
    near, far = count(sizes, NEAR), count(sizes, FAR)
    rows = parts.shape[0]
    mine = exchange(parts.reshape(near, rows // near, LANES), NEAR)
    mine = exchange(combine(mine, far), FAR)
    return exchange(combine(mine, near), NEAR).reshape(rows, LANES)


def over_sources(mine, other, sizes):
    group = count(sizes, CHIPS)
    rows = mine.shape[0]
    mine = join(mine, lax.all_gather(other, "core"))
    mine = exchange(mine.reshape(group, rows // group, LANES), CHIPS)
    half = exchange(combine(mine, group), CHIPS).reshape(rows, LANES)
    return lax.all_gather(half, "core").reshape(2 * rows, LANES)


def body(sizes, source, target, log_source, log_target):
    source, target = source.T, target.T
    parts, *kept, target_norms, source_norms, log_target, log_source = first_update(
        target, source, log_target, log_source
    )
    for step in range(ITERS):
        if step:
            (parts,) = next_update(source, target, log_target, target_known, kept, True)
        source_known = over_targets(parts, sizes)
        target_known = over_sources(*next_update(target, source, log_source, source_known, kept, False), sizes)
    return finish(source_known, source_norms, target_known, target_norms)


def solution(mesh):
    sizes = {"yh": 2, "x": 4, "core": 2, "z3": 2, "z2": 2, "z1": 2, "z0": 2, "yl": 2}
    fine = Mesh(mesh.devices.reshape(tuple(sizes.values())), tuple(sizes))
    src, tgt = ("yh", "x", "core"), ("z3", "z2", "z1", "z0", "yl")
    in_specs = (P(src, None), P(tgt, None), P(None, src), P(None, tgt))
    out_specs = (P(None, src), P(None, tgt))
    return jax.shard_map(
        functools.partial(body, sizes), mesh=fine, in_specs=in_specs, out_specs=out_specs, check_vma=False
    )
```
